512 devices in a mesh: depth: 8 (over z_lo, core), lat: 64 (over z_hi, x, y).
Axes of the slice: x: 4, y: 8, z: 8 (z_hi: 2, z_lo: 4; z = z_hi * 4 + z_lo), core: 2. Of those that a mesh axis runs over, the one named last changes fastest.
Arguments:
- forcing: bfloat16 [8, 2, 16, 16384], P('depth', None, None, 'lat'), may hold values from -6 to 6
- blocks: bfloat16 [8, 768, 2, 128, 128], P('depth', 'lat'), may hold values from -0.15625 to 0.15625
- block_rows: int32 [8, 768], P('depth', 'lat'), may hold values from 0 to 1
- block_cols: int32 [8, 768], P('depth', 'lat'), may hold values from 0 to 5
Outputs:
- down_traces: bfloat16 [8, 2, 16, 16384], P('depth', None, None, 'lat')
- up_traces: bfloat16 [8, 2, 16, 16384], P('depth', None, None, 'lat')
The draws below stay inside these ranges and needn't reach their ends.
Inputs may be any that keep to these rules, and one draw needn't show every extreme that they name: `block_rows`: a block row index inside the owner's own block rows. `block_cols`: below 2: the previous lateral device's block rows; from 4: the next device's.
All inputs are finite; a program needn't handle non-finite values.
Results may differ from the reference program's by a relative error of at most 0.025.
Values may be sent and summed in bfloat16 or wider, within the bound.
No kernel may reach another device: no remote copies, remote signals or barrier semaphores. Data moves between devices by JAX's collectives and lax.ppermute only.
A program may use at most 64 MiB of HBM per device.

```python
import jax
import jax.numpy as jnp

BLK = 128
SRC = 16
PER_ROW = 6
RB_DEV = 2
LAYERS = 8
NB_DEV = 12
NBT = 768
PLANE = 16384
N_LAT = 64


def place_ends(values, key, least, high):
    longest = values.shape.index(max(values.shape))
    spots = []
    for shift in (0, 1):
        where = [jax.random.randint(jax.random.fold_in(key, axis), (), 0, length) for axis, length in enumerate(values.shape)]
        where[longest] = (where[longest] + shift) % values.shape[longest]
        spots.append(tuple(where))
    return values.at[spots[0]].set(least).at[spots[1]].set(high)


def levels(rng, shape, cuts, low, high):
    def one(dim, blocks):
        heights = jax.random.uniform(jax.random.fold_in(jax.random.fold_in(rng, 6), dim), (blocks,), jnp.float32, low / len(cuts), high / len(cuts))
        return jnp.repeat(jnp.exp(heights), shape[dim] // blocks).reshape((-1,) + (1,) * (len(shape) - dim - 1))

    factor_of = one(*cuts[0])
    for cut in cuts[1:]:
        factor_of = factor_of * one(*cut)
    return factor_of


def noise(rng, dims, deviation, limit, split=(), held_as=jnp.bfloat16):
    entries = deviation * jax.random.normal(rng, dims, jnp.float32)
    if split:
        entries = entries * levels(rng, dims, split, -0.22, 0.18)
    return jnp.clip(entries, -limit, limit).astype(held_as)


def setup_inputs(seed: int = 0) -> dict:
    key_list = jax.random.split(jax.random.key(seed), 5)
    return {
        "forcing": noise(key_list[0], (LAYERS, 2, SRC, PLANE), 1.0, 6.0, ((0, 8), (3, 64))),
        "blocks": noise(key_list[1], (LAYERS, NBT, 2, BLK, BLK), (2 * BLK * PER_ROW) ** -0.5, 0.15625, ((0, 8), (1, 64))),
        "block_rows": place_ends(jax.random.randint(key_list[2], (LAYERS, NBT), 0, RB_DEV), jax.random.fold_in(key_list[2], 1), 0, RB_DEV - 1).astype(jnp.int32),
        "block_cols": place_ends(jax.random.randint(key_list[3], (LAYERS, NBT), 0, 3 * RB_DEV), jax.random.fold_in(key_list[3], 1), 0, (3 * RB_DEV) - 1).astype(jnp.int32),
    }


def apply_layer(layer_blocks, rows_index, cols_index, field):
    total_blocks = layer_blocks.shape[0]
    owner = jnp.arange(total_blocks, dtype=jnp.int32) // NB_DEV
    global_rows = (owner * RB_DEV + rows_index).astype(jnp.int32)
    global_cols = (owner * RB_DEV + cols_index).astype(jnp.int32)
    padded = jnp.pad(field, ((0, 0), (0, 0), (RB_DEV, RB_DEV), (0, 0)))
    picked = jnp.take(padded, global_cols, axis=2).astype(jnp.float32)
    product = jnp.einsum("bpij,qsbj->pqsbi", layer_blocks.astype(jnp.float32), picked)
    combined = jnp.stack([product[0, 0] - product[1, 1], product[0, 1] + product[1, 0]])
    summed = jax.ops.segment_sum(jnp.moveaxis(combined, 2, 0), global_rows, num_segments=RB_DEV * N_LAT)
    return jnp.moveaxis(summed, 0, 2)


def reference(forcing, blocks, block_rows, block_cols):
    layers = forcing.shape[0]
    shaped = forcing.reshape(layers, 2, SRC, RB_DEV * N_LAT, BLK)
    from_above = jnp.zeros(shaped.shape[1:], jnp.bfloat16)
    aboves = []
    downs = []
    for layer in range(layers):
        operand = (shaped[layer].astype(jnp.float32) + from_above.astype(jnp.float32)).astype(jnp.bfloat16)
        result = apply_layer(blocks[layer], block_rows[layer], block_cols[layer], operand).astype(jnp.bfloat16)
        aboves.append(from_above)
        downs.append(result)
        from_above = result
    from_below = jnp.zeros(shaped.shape[1:], jnp.bfloat16)
    ups = [None] * layers
    for layer in reversed(range(layers)):
        operand = (shaped[layer].astype(jnp.float32) + aboves[layer].astype(jnp.float32) + from_below.astype(jnp.float32)).astype(jnp.bfloat16)
        result = apply_layer(blocks[layer], block_rows[layer], block_cols[layer], operand).astype(jnp.bfloat16)
        ups[layer] = result
        from_below = result
    down_traces = jnp.stack(downs).reshape(forcing.shape)
    up_traces = jnp.stack(ups).reshape(forcing.shape)
    return (down_traces, up_traces)
```

```python
import functools

import jax
import jax.numpy as jnp
from jax import lax
from jax.experimental import pallas as pl
from jax.experimental.pallas import tpu as pltpu
from jax.sharding import PartitionSpec as P

AXES = ("depth", "lat")
FAR, NEAR, SAME = range(3)
PARAMS = pltpu.CompilerParams(vmem_limit_bytes=16 * 2**20)


def gather_kernel(rows_ref, cols_ref, blocks_ref, dense_ref, total_ref):
    count, parts, size, _ = blocks_ref.shape
    rows, slots = total_ref.shape[:2]
    total_ref[...] = jnp.zeros_like(total_ref)
    for b in range(count):
        total_ref[rows_ref[0, b], cols_ref[0, b]] += blocks_ref[b].astype(jnp.float32)
    for r in range(rows):
        for s in range(slots):
            for p in range(parts):
                column = (p * rows + r) * size
                dense_ref[s * size : (s + 1) * size, column : column + size] = (
                    total_ref[r, s, p].T.astype(jnp.bfloat16)
                )


def applied(order, first_ref, second_ref, third_ref, dense_ref):
    sources, width = first_ref.shape[1:]
    refs = dict(zip(order, (first_ref, second_ref, third_ref)))
    window = jnp.concatenate(
        [refs[part][...].reshape(2 * sources, width) for part in (FAR, SAME, NEAR)], axis=1
    )
    product = jnp.dot(window, dense_ref[...], preferred_element_type=jnp.float32)
    by_real, by_imag = product[:, :width], product[:, width:]
    real = by_real[:sources] - by_imag[sources:]
    imag = by_real[sources:] + by_imag[:sources]
    return real, imag


def down_kernel(layer, order, first_ref, second_ref, third_ref, dense_ref, kept_ref, next_ref, send_ref, down_ref):
    down_ref[...] = kept_ref[...]

    @pl.when(lax.axis_index("depth") == layer)
    def _():
        for part, total in enumerate(applied(order, first_ref, second_ref, third_ref, dense_ref)):
            trace = total.astype(jnp.bfloat16).astype(jnp.float32)
            down_ref[part] = total
            send_ref[part] = (next_ref[part].astype(jnp.float32) + trace).astype(jnp.bfloat16)


def turn_kernel(layer, order, first_ref, second_ref, third_ref, dense_ref, kept_ref, send_ref, down_ref):
    down_ref[...] = kept_ref[...]

    @pl.when(lax.axis_index("depth") == layer)
    def _():
        for part, total in enumerate(applied(order, first_ref, second_ref, third_ref, dense_ref)):
            down_ref[part] = total
            send_ref[part] = total.astype(jnp.bfloat16)


def up_kernel(layer, order, first_ref, second_ref, third_ref, dense_ref, down_ref, kept_ref, send_ref, up_ref):
    up_ref[...] = kept_ref[...]

    @pl.when(lax.axis_index("depth") == layer)
    def _():
        for part, total in enumerate(applied(order, first_ref, second_ref, third_ref, dense_ref)):
            total = down_ref[part] + total
            up_ref[part] = total
            send_ref[part] = total.astype(jnp.bfloat16)


def vmem(count):
    return [pl.BlockSpec(memory_space=pltpu.VMEM)] * count


def local(forcing, blocks, block_rows, block_cols):
    layers, lats = lax.axis_size("depth"), lax.axis_size("lat")
    field = forcing[0]
    _, sources, width = field.shape
    count, parts, size, _ = blocks.shape[1:]
    rows = width // size

    def sent(value, moves):
        pairs = [
            (k * lats + j, to_k * lats + to_j)
            for k, j, to_k, to_j in moves
            if 0 <= to_k < layers and 0 <= to_j < lats
        ]
        return lax.ppermute(value, AXES, pairs)

    def beside(j, odd):
        return j + 1 if (j % 2 == 1) == odd else j - 1

    def far(value, k, to_k):
        return sent(value, [(k, j, to_k, beside(j, True)) for j in range(lats)])

    def near(value, k, to_k):
        return sent(value, [(k, j, to_k, beside(j, False)) for j in range(lats)])

    def same(value, k, to_k):
        return sent(value, [(k, j, to_k, j) for j in range(lats)])

    following = sent(field, [(k, j, k - 1, j) for k in range(1, layers) for j in range(lats)])

    left_is_far = lax.axis_index("lat") % 2 == 0
    cols = jnp.where(left_is_far, block_cols, 2 * rows - block_cols // rows * rows + block_cols % rows)
    dense = pl.pallas_call(
        gather_kernel,
        out_shape=jax.ShapeDtypeStruct((3 * width, parts * width), jnp.bfloat16),
        in_specs=[pl.BlockSpec(memory_space=pltpu.SMEM)] * 2 + vmem(1),
        out_specs=pl.BlockSpec(memory_space=pltpu.VMEM),
        scratch_shapes=[pltpu.VMEM((rows, 3 * rows, parts, size, size), jnp.float32)],
        compiler_params=PARAMS,
        name="dense",
    )(block_rows, cols, blocks[0])

    half = jax.ShapeDtypeStruct(field.shape, jnp.bfloat16)
    full = jax.ShapeDtypeStruct(field.shape, jnp.float32)

    def step(kernel, layer, order, *operands):
        return pl.pallas_call(
            functools.partial(kernel, layer, order),
            out_shape=(half, full),
            in_specs=vmem(len(operands)),
            out_specs=tuple(vmem(2)),
            compiler_params=PARAMS,
            name=f"{kernel.__name__}{layer}",
        )(*operands)

    def moved(value, k, to_k, order):
        parts = {FAR: far, NEAR: near, SAME: same}
        return [parts[part](value, k, to_k) for part in order]

    last = layers - 1
    down = jnp.zeros(field.shape, jnp.float32)
    order, window = (FAR, NEAR, SAME), [far(field, 0, 0), near(field, 0, 0), field]
    for layer in range(last):
        send, down = step(down_kernel, layer, order, *window, dense, down, following)
        order = (SAME, FAR, NEAR) if layer == 2 else (FAR, NEAR, SAME)
        window = moved(send, layer, layer + 1, order)
    send, down = step(turn_kernel, last, order, *window, dense, down)
    up = down
    for layer in reversed(range(last)):
        window = moved(send, layer + 1, layer, order)
        send, up = step(up_kernel, layer, order, *window, dense, down, up)
    down, up = down.astype(jnp.bfloat16), up.astype(jnp.bfloat16)
    return (down.reshape(forcing.shape), up.reshape(forcing.shape))


def solution(mesh):
    placed = (
        P("depth", None, None, "lat"),
        P("depth", "lat", None, None, None),
        P("depth", "lat"),
        P("depth", "lat"),
    )
    return jax.shard_map(
        local,
        mesh=mesh,
        in_specs=placed,
        out_specs=(P("depth", None, None, "lat"), P("depth", None, None, "lat")),
        check_vma=False,
    )
```

```python
import functools

import jax
import jax.numpy as jnp
from jax import lax
from jax.experimental import pallas as pl
from jax.experimental.pallas import tpu as pltpu
from jax.sharding import PartitionSpec as P

AXES = ("depth", "lat")
FAR, NEAR, SAME = range(3)
PARAMS = pltpu.CompilerParams(vmem_limit_bytes=16 * 2**20)


def gather_kernel(rows_ref, cols_ref, blocks_ref, dense_ref, total_ref):
    count, parts, size, _ = blocks_ref.shape
    rows, slots = total_ref.shape[:2]
    total_ref[...] = jnp.zeros_like(total_ref)
    for b in range(count):
        total_ref[rows_ref[0, b], cols_ref[0, b]] += blocks_ref[b].astype(jnp.float32)
    for r in range(rows):
        for s in range(slots):
            for p in range(parts):
                column = (p * rows + r) * size
                dense_ref[s * size : (s + 1) * size, column : column + size] = (
                    total_ref[r, s, p].T.astype(jnp.bfloat16)
                )


def applied(order, first_ref, second_ref, third_ref, dense_ref):
    sources, width = first_ref.shape[1:]
    refs = dict(zip(order, (first_ref, second_ref, third_ref)))
    window = jnp.concatenate(
        [refs[part][...].reshape(2 * sources, width) for part in (FAR, SAME, NEAR)], axis=1
    )
    product = jnp.dot(window, dense_ref[...], preferred_element_type=jnp.float32)
    by_real, by_imag = product[:, :width], product[:, width:]
    real = by_real[:sources] - by_imag[sources:]
    imag = by_real[sources:] + by_imag[:sources]
    return real, imag


def down_kernel(layer, order, first_ref, second_ref, third_ref, dense_ref, kept_ref, next_ref, send_ref, down_ref):
    down_ref[...] = kept_ref[...]

    @pl.when(lax.axis_index("depth") == layer)
    def _():
        for part, total in enumerate(applied(order, first_ref, second_ref, third_ref, dense_ref)):
            trace = total.astype(jnp.bfloat16).astype(jnp.float32)
            down_ref[part] = total
            send_ref[part] = (next_ref[part].astype(jnp.float32) + trace).astype(jnp.bfloat16)


def turn_kernel(layer, order, first_ref, second_ref, third_ref, dense_ref, kept_ref, send_ref, down_ref):
    down_ref[...] = kept_ref[...]

    @pl.when(lax.axis_index("depth") == layer)
    def _():
        for part, total in enumerate(applied(order, first_ref, second_ref, third_ref, dense_ref)):
            down_ref[part] = total
            send_ref[part] = total.astype(jnp.bfloat16)


def up_kernel(layer, order, first_ref, second_ref, third_ref, dense_ref, down_ref, kept_ref, send_ref, up_ref):
    up_ref[...] = kept_ref[...]

    @pl.when(lax.axis_index("depth") == layer)
    def _():
        for part, total in enumerate(applied(order, first_ref, second_ref, third_ref, dense_ref)):
            total = down_ref[part] + total
            up_ref[part] = total
            send_ref[part] = total.astype(jnp.bfloat16)


def vmem(count):
    return [pl.BlockSpec(memory_space=pltpu.VMEM)] * count


def local(forcing, blocks, block_rows, block_cols):
    layers, lats = lax.axis_size("depth"), lax.axis_size("lat")
    field = forcing[0]
    _, sources, width = field.shape
    count, parts, size, _ = blocks.shape[1:]
    rows = width // size

    def sent(value, moves):
        pairs = [
            (k * lats + j, to_k * lats + to_j)
            for k, j, to_k, to_j in moves
            if 0 <= to_k < layers and 0 <= to_j < lats
        ]
        return lax.ppermute(value, AXES, pairs)

    def beside(j, odd):
        return j + 1 if (j % 2 == 1) == odd else j - 1

    def far(value, k, to_k):
        return sent(value, [(k, j, to_k, beside(j, True)) for j in range(lats)])

    def rounds(k, to_k):
        half = layers // 2
        return [(i, i + to_k - k) for i in range(k % half, layers, half)]

    def near(value, k, to_k):
        return sent(value, [(i, j, to_i, beside(j, False)) for i, to_i in rounds(k, to_k) for j in range(lats)])

    def same(value, k, to_k):
        return sent(value, [(i, j, to_i, j) for i, to_i in rounds(k, to_k) for j in range(lats)])

    following = sent(field, [(k, j, k - 1, j) for k in range(1, layers) for j in range(lats)])

    left_is_far = lax.axis_index("lat") % 2 == 0
    cols = jnp.where(left_is_far, block_cols, 2 * rows - block_cols // rows * rows + block_cols % rows)
    dense = pl.pallas_call(
        gather_kernel,
        out_shape=jax.ShapeDtypeStruct((3 * width, parts * width), jnp.bfloat16),
        in_specs=[pl.BlockSpec(memory_space=pltpu.SMEM)] * 2 + vmem(1),
        out_specs=pl.BlockSpec(memory_space=pltpu.VMEM),
        scratch_shapes=[pltpu.VMEM((rows, 3 * rows, parts, size, size), jnp.float32)],
        compiler_params=PARAMS,
        name="dense",
    )(block_rows, cols, blocks[0])

    half = jax.ShapeDtypeStruct(field.shape, jnp.bfloat16)
    full = jax.ShapeDtypeStruct(field.shape, jnp.float32)

    def step(kernel, layer, order, *operands):
        return pl.pallas_call(
            functools.partial(kernel, layer, order),
            out_shape=(half, full),
            in_specs=vmem(len(operands)),
            out_specs=tuple(vmem(2)),
            compiler_params=PARAMS,
            name=f"{kernel.__name__}{layer}",
        )(*operands)

    def moved(value, k, to_k, order):
        parts = {FAR: far, NEAR: near, SAME: same}
        return [parts[part](value, k, to_k) for part in order]

    last = layers - 1
    down = jnp.zeros(field.shape, jnp.float32)
    order, window = (FAR, NEAR, SAME), [far(field, 0, 0), sent(field, [(0, j, 0, beside(j, False)) for j in range(lats)]), field]
    for layer in range(last):
        send, down = step(down_kernel, layer, order, *window, dense, down, following)
        order = (SAME, FAR, NEAR) if layer == 2 else (FAR, NEAR, SAME)
        window = moved(send, layer, layer + 1, order)
    send, down = step(turn_kernel, last, order, *window, dense, down)
    up = down
    for layer in reversed(range(last)):
        window = moved(send, layer + 1, layer, order)
        send, up = step(up_kernel, layer, order, *window, dense, down, up)
    down, up = down.astype(jnp.bfloat16), up.astype(jnp.bfloat16)
    return (down.reshape(forcing.shape), up.reshape(forcing.shape))


def solution(mesh):
    placed = (
        P("depth", None, None, "lat"),
        P("depth", "lat", None, None, None),
        P("depth", "lat"),
        P("depth", "lat"),
    )
    return jax.shard_map(
        local,
        mesh=mesh,
        in_specs=placed,
        out_specs=(P("depth", None, None, "lat"), P("depth", None, None, "lat")),
        check_vma=False,
    )
```

```python
import functools

import jax
import jax.numpy as jnp
from jax import lax
from jax.experimental import pallas as pl
from jax.experimental.pallas import tpu as pltpu
from jax.sharding import PartitionSpec as P

AXES = ("depth", "lat")
PARAMS = pltpu.CompilerParams(vmem_limit_bytes=24 * 2**20)


def dense_kernel(rows_ref, cols_ref, blocks_ref, dense_ref, total_ref):
    count, parts, size, _ = blocks_ref.shape
    rows, slots = total_ref.shape[:2]
    total_ref[...] = jnp.zeros_like(total_ref)
    for b in range(count):
        total_ref[rows_ref[0, b], cols_ref[0, b]] += blocks_ref[b].astype(jnp.float32)
    for r in range(rows):
        for s in range(slots):
            for p in range(parts):
                column = (p * rows + r) * size
                dense_ref[s * size : (s + 1) * size, column : column + size] = (
                    total_ref[r, s, p].T.astype(jnp.bfloat16)
                )


def hold_kernel(field_ref, *refs):
    refs[-1][...] = field_ref[...]


def later_kernel(layers, dense_ref, _after, copy_ref):
    layer = lax.axis_index("depth")

    @pl.when(functools.reduce(jnp.logical_or, [layer == k for k in layers]))
    def _():
        copy_ref[...] = dense_ref[...]


def up_kernel(layer, far_ref, near_ref, same_ref, dense_ref, down_ref, kept_ref, up_ref):
    up_ref[...] = kept_ref[...]

    @pl.when(lax.axis_index("depth") == layer)
    def _():
        window = (far_ref[...], same_ref[...], near_ref[...])
        up_ref[...] = plus(down_ref[...], applied(window, dense_ref))


def applied(window, dense_ref):
    sources, width = window[0].shape[1:]
    flat = jnp.concatenate([part.reshape(2 * sources, width) for part in window], axis=1)
    product = jnp.dot(flat, dense_ref[...], preferred_element_type=jnp.float32)
    by_real, by_imag = product[:, :width], product[:, width:]
    real = by_real[:sources] - by_imag[sources:]
    imag = by_real[sources:] + by_imag[:sources]
    return jnp.stack([real, imag])


def plus(field, trace):
    return (field.astype(jnp.float32) + trace.astype(jnp.float32)).astype(jnp.bfloat16)


def three(outer, far_ref, near_ref, same_ref, dense_refs, pairs_ref):
    first_ref, second_ref = outer
    place = lax.axis_index("lat") % 4
    first_is_far = (place == 0) | (place == 3)

    @pl.when(first_is_far)
    def _():
        pairs_ref[0] = first_ref[...]
        pairs_ref[1] = second_ref[...]

    @pl.when(jnp.logical_not(first_is_far))
    def _():
        pairs_ref[0] = second_ref[...]
        pairs_ref[1] = first_ref[...]

    far, near, same = far_ref[...], near_ref[...], same_ref[...]
    return (
        applied((same, far, pairs_ref[0]), dense_refs[0]),
        applied((far, same, near), dense_refs[1]),
        applied((pairs_ref[1], near, same), dense_refs[2]),
    )


def down_kernel(layer, next_ref, far_ref, near_ref, same_ref, dense_ref, kept_ref, sent_ref, send_ref, down_ref):
    down_ref[...] = kept_ref[...]
    send_ref[...] = sent_ref[...]

    @pl.when(lax.axis_index("depth") == layer)
    def _():
        window = (far_ref[...], same_ref[...], near_ref[...])
        trace = applied(window, dense_ref).astype(jnp.bfloat16)
        down_ref[...] = trace
        send_ref[...] = plus(next_ref[...], trace)


def down_two_kernel(
    layer, first_ref, far_ref, second_ref, near_ref, same_ref, other_far_ref, other_same_ref, other_near_ref,
    dense_ref, field_far_ref, field_ref, field_near_ref, kept_ref, down_ref, both_ref, pairs_ref,
):
    down_ref[...] = kept_ref[...]

    @pl.when(lax.axis_index("depth") == layer)
    def _():
        others = (other_far_ref, other_same_ref, other_near_ref)
        traces = [
            total.astype(jnp.bfloat16)
            for total in three((first_ref, second_ref), far_ref, near_ref, same_ref, others, pairs_ref)
        ]
        fields = (field_far_ref[...], field_ref[...], field_near_ref[...])
        window = [plus(field, trace) for field, trace in zip(fields, traces)]
        trace = applied(window, dense_ref).astype(jnp.bfloat16)
        down_ref[...] = trace
        both_ref[1] = traces[1]

    both_ref[0] = down_ref[...]


def turn_kernel(layer, far_ref, near_ref, both_ref, dense_ref, wait_ref, kept_ref, send_ref, up_ref, down_ref):
    up_ref[...] = kept_ref[...]
    down_ref[...] = kept_ref[...]

    @pl.when(lax.axis_index("depth") == layer)
    def _():
        down_ref[...] = both_ref[1]
        window = (far_ref[0], both_ref[0], near_ref[0])
        trace = plus(both_ref[1], applied(window, dense_ref))
        up_ref[...] = trace
        send_ref[...] = plus(wait_ref[...], trace)


def up_two_kernel(
    layer, waits, first_ref, far_ref, second_ref, near_ref, same_ref, other_far_ref, other_same_ref, other_near_ref,
    dense_ref, down_ref, wait_ref, kept_ref, other_ref, send_ref, up_ref, back_ref, pairs_ref,
):
    up_ref[...] = kept_ref[...]
    back_ref[...] = other_ref[...]

    @pl.when(lax.axis_index("depth") == layer)
    def _():
        others = (other_far_ref, other_same_ref, other_near_ref)
        totals = three((first_ref, second_ref), far_ref, near_ref, same_ref, others, pairs_ref)
        window = [total.astype(jnp.bfloat16) for total in totals]
        back_ref[...] = window[1]
        trace = plus(down_ref[...], applied(window, dense_ref))
        up_ref[...] = trace
        send_ref[...] = plus(wait_ref[...], trace) if waits else trace


def end_kernel(layers, up_ref, returned_ref, out_ref):
    layer = lax.axis_index("depth")
    elsewhere = functools.reduce(jnp.logical_or, [layer == k for k in layers])

    @pl.when(elsewhere)
    def _():
        out_ref[...] = returned_ref[...]

    @pl.when(jnp.logical_not(elsewhere))
    def _():
        out_ref[...] = up_ref[...]


def vmem(count):
    return [pl.BlockSpec(memory_space=pltpu.VMEM)] * count


def local(forcing, blocks, block_rows, block_cols):
    layers, lats = lax.axis_size("depth"), lax.axis_size("lat")
    field = forcing[0]
    _, sources, width = field.shape
    count, parts, size, _ = blocks.shape[1:]
    rows = width // size
    top = layers - 1

    def sent(value, steps, place):
        pairs = [
            (k * lats + j, to_k * lats + place(j))
            for k, to_k in steps
            for j in range(lats)
            if 0 <= place(j) < lats
        ]
        return lax.ppermute(value, AXES, pairs)

    def far(j):
        return j + 1 if j % 2 else j - 1

    def near(j):
        return j - 1 if j % 2 else j + 1

    def same(j):
        return j

    def first(j):
        return j + 2 if j % 4 > 1 else j - 2

    def second(j):
        return j - 2 if j % 4 > 1 else j + 2

    rounds = [(k, k + 1) for k in range(top - 2)]
    rounds += [(top - 2, top), (top, top - 1)] + [(k, k - 2) for k in range(top - 1, 2, -2)] + [(2, 1), (1, 0)]
    wide, narrow = {step: [step] for step in rounds}, {step: [step] for step in rounds}
    if layers == 8:
        for shared in ([(0, 1), (3, 4)], [(1, 2), (4, 5)], [(2, 3), (7, 6)]):
            narrow |= {step: shared for step in shared}
        for shared in ([(5, 7), (4, 2)],):
            narrow |= {step: shared for step in shared}
            wide |= {step: shared for step in shared}

    def moved(value, k, to_k):
        step = narrow[k, to_k]
        return sent(value, [(k, to_k)], far), sent(value, step, near), sent(value, step, same)

    def moved_two(value, k, to_k):
        outer, inner = wide[k, to_k], narrow[k, to_k]
        return (
            sent(value, outer, first),
            sent(value, outer, far),
            sent(value, outer, second),
            sent(value, inner, near),
            sent(value, inner, same),
        )

    following = sent(field, [(k, k - 1) for k in range(1, layers)], same)
    beside = [(0, 0), (top, top)]
    field_far, field_near = sent(field, beside, far), sent(field, beside, near)

    left_is_far = lax.axis_index("lat") % 2 == 0
    cols = jnp.where(left_is_far, block_cols, 2 * rows - block_cols // rows * rows + block_cols % rows)
    matrix = jax.ShapeDtypeStruct((3 * width, parts * width), jnp.bfloat16)
    dense = pl.pallas_call(
        dense_kernel,
        out_shape=matrix,
        in_specs=[pl.BlockSpec(memory_space=pltpu.SMEM)] * 2 + vmem(1),
        out_specs=pl.BlockSpec(memory_space=pltpu.VMEM),
        scratch_shapes=[pltpu.VMEM((rows, 3 * rows, parts, size, size), jnp.float32)],
        compiler_params=PARAMS,
        name="dense",
    )(block_rows, cols, blocks[0])

    one = jax.ShapeDtypeStruct(field.shape, jnp.bfloat16)
    two = jax.ShapeDtypeStruct((2, *field.shape), jnp.bfloat16)

    def step(kernel, out_shape, layer, *operands, pairs=False):
        return pl.pallas_call(
            functools.partial(kernel, *layer),
            out_shape=out_shape,
            in_specs=vmem(len(operands)),
            out_specs=tuple(vmem(len(out_shape))),
            scratch_shapes=[pltpu.VMEM(two.shape, two.dtype)] if pairs else [],
            compiler_params=PARAMS,
            name=kernel.__name__,
        )(*operands)

    def hold(value, *others):
        return pl.pallas_call(
            hold_kernel,
            out_shape=one,
            in_specs=vmem(1) + [pl.BlockSpec(memory_space=pl.ANY)] * len(others),
            out_specs=pl.BlockSpec(memory_space=pltpu.VMEM),
            compiler_params=PARAMS,
            name="hold",
        )(value, *others)

    ups = [(k + 1, k) for k in range(2, top - 1, 2)]
    given = [*ups, (top - 1, top)]
    send = down = jnp.zeros(field.shape, jnp.bfloat16)
    window = (field_far, field_near, field)
    for layer in range(top - 1):
        if layer == 1:
            following = hold(following, other_same)
        if layer == 4:
            following = hold(following, other_far, other_near)
        send, down = step(down_kernel, (one, one), (layer,), following, *window, dense, down, send)
        if layer == 0:
            [copy] = step(later_kernel, (matrix,), ([k for k, _ in given],), dense, send)
            other_far, other_near, other_same = (sent(copy, given, place) for place in (far, near, same))
        if layer == top - 3:
            wait = sent(send, [(k, k + 2) for k in range(2, top - 2, 2)], same)
        if layer + 1 < top - 1:
            window = moved(send, layer, layer + 1)
    window = moved_two(send, top - 2, top)
    down, both = step(
        down_two_kernel, (one, two), (top,), *window, other_far, other_same, other_near, dense,
        field_far, field, field_near, down, pairs=True,
    )
    window = moved(both, top, top - 1)
    send, up, down = step(turn_kernel, (one,) * 3, (top - 1,), *window, dense, wait, down)
    back = jnp.zeros(field.shape, jnp.bfloat16)
    for layer in range(top - 3, 1, -2):
        window = moved_two(send, layer + 2, layer)
        send, up, back = step(
            up_two_kernel, (one,) * 3, (layer, layer > 2), *window, other_far, other_same, other_near, dense,
            down, wait, up, back, pairs=True,
        )
    returned = sent(back, [(to_k, k) for k, to_k in ups], same)
    [up] = step(up_kernel, (one,), (1,), *moved(send, 2, 1), dense, down, up)
    [up] = step(end_kernel, (one,), ([k for k, _ in ups],), up, returned)
    [up] = step(up_kernel, (one,), (0,), *moved(up, 1, 0), dense, down, up)
    return (down.reshape(forcing.shape), up.reshape(forcing.shape))


def solution(mesh):
    placed = (
        P("depth", None, None, "lat"),
        P("depth", "lat", None, None, None),
        P("depth", "lat"),
        P("depth", "lat"),
    )
    return jax.shard_map(
        local,
        mesh=mesh,
        in_specs=placed,
        out_specs=(P("depth", None, None, "lat"), P("depth", None, None, "lat")),
        check_vma=False,
    )
```

```python
import functools

import jax
import jax.numpy as jnp
from jax import lax
from jax.experimental import pallas as pl
from jax.experimental.pallas import tpu as pltpu
from jax.sharding import PartitionSpec as P

AXES = ("depth", "lat")
PARAMS = pltpu.CompilerParams(vmem_limit_bytes=24 * 2**20)


def dense_kernel(rows_ref, cols_ref, blocks_ref, dense_ref, total_ref):
    count, parts, size, _ = blocks_ref.shape
    rows, slots = total_ref.shape[:2]
    total_ref[...] = jnp.zeros_like(total_ref)
    for b in range(count):
        total_ref[rows_ref[0, b], cols_ref[0, b]] += blocks_ref[b].astype(jnp.float32)
    for r in range(rows):
        for s in range(slots):
            for p in range(parts):
                column = (p * rows + r) * size
                dense_ref[s * size : (s + 1) * size, column : column + size] = (
                    total_ref[r, s, p].T.astype(jnp.bfloat16)
                )


def hold_kernel(field_ref, *refs):
    refs[-1][...] = field_ref[...]


def later_kernel(layers, dense_ref, _after, copy_ref):
    layer = lax.axis_index("depth")

    @pl.when(functools.reduce(jnp.logical_or, [layer == k for k in layers]))
    def _():
        copy_ref[...] = dense_ref[...]


def up_kernel(layer, far_ref, near_ref, same_ref, dense_ref, down_ref, kept_ref, up_ref):
    up_ref[...] = kept_ref[...]

    @pl.when(lax.axis_index("depth") == layer)
    def _():
        window = (far_ref[...], same_ref[...], near_ref[...])
        up_ref[...] = plus(down_ref[...], applied(window, dense_ref))


def applied(window, dense_ref):
    sources, width = window[0].shape[1:]
    flat = jnp.concatenate([part.reshape(2 * sources, width) for part in window], axis=1)
    product = jnp.dot(flat, dense_ref[...], preferred_element_type=jnp.float32)
    by_real, by_imag = product[:, :width], product[:, width:]
    real = by_real[:sources] - by_imag[sources:]
    imag = by_real[sources:] + by_imag[:sources]
    return jnp.stack([real, imag])


def plus(field, trace):
    return (field.astype(jnp.float32) + trace.astype(jnp.float32)).astype(jnp.bfloat16)


def three(outer, far_ref, near_ref, same_ref, dense_refs, pairs_ref):
    first_ref, second_ref = outer
    place = lax.axis_index("lat") % 4
    first_is_far = (place == 0) | (place == 3)

    @pl.when(first_is_far)
    def _():
        pairs_ref[0] = first_ref[...]
        pairs_ref[1] = second_ref[...]

    @pl.when(jnp.logical_not(first_is_far))
    def _():
        pairs_ref[0] = second_ref[...]
        pairs_ref[1] = first_ref[...]

    far, near, same = far_ref[...], near_ref[...], same_ref[...]
    return (
        applied((same, far, pairs_ref[0]), dense_refs[0]),
        applied((far, same, near), dense_refs[1]),
        applied((pairs_ref[1], near, same), dense_refs[2]),
    )


def down_kernel(layer, next_ref, far_ref, near_ref, same_ref, dense_ref, kept_ref, sent_ref, send_ref, down_ref):
    down_ref[...] = kept_ref[...]
    send_ref[...] = sent_ref[...]

    @pl.when(lax.axis_index("depth") == layer)
    def _():
        window = (far_ref[...], same_ref[...], near_ref[...])
        trace = applied(window, dense_ref).astype(jnp.bfloat16)
        down_ref[...] = trace
        send_ref[...] = plus(next_ref[...], trace)


def down_two_kernel(
    layer, first_ref, far_ref, second_ref, near_ref, same_ref, other_far_ref, other_same_ref, other_near_ref,
    dense_ref, field_far_ref, field_ref, field_near_ref, next_ref, kept_ref, sent_ref,
    send_ref, down_ref, wait_ref, both_ref, pairs_ref,
):
    down_ref[...] = kept_ref[...]
    wait_ref[...] = sent_ref[...]

    @pl.when(lax.axis_index("depth") == layer)
    def _():
        others = (other_far_ref, other_same_ref, other_near_ref)
        traces = [
            total.astype(jnp.bfloat16)
            for total in three((first_ref, second_ref), far_ref, near_ref, same_ref, others, pairs_ref)
        ]
        fields = (field_far_ref[...], field_ref[...], field_near_ref[...])
        window = [plus(field, trace) for field, trace in zip(fields, traces)]
        trace = applied(window, dense_ref).astype(jnp.bfloat16)
        down_ref[...] = trace
        send_ref[...] = plus(next_ref[...], trace)
        wait_ref[...] = window[1]
        both_ref[0] = trace
        both_ref[1] = traces[1]


def turn_kernel(layer, far_ref, near_ref, both_ref, dense_ref, wait_ref, kept_ref, send_ref, up_ref, down_ref):
    up_ref[...] = kept_ref[...]
    down_ref[...] = kept_ref[...]

    @pl.when(lax.axis_index("depth") == layer)
    def _():
        down_ref[...] = both_ref[1]
        window = (far_ref[0], both_ref[0], near_ref[0])
        trace = plus(both_ref[1], applied(window, dense_ref))
        up_ref[...] = trace
        send_ref[...] = plus(wait_ref[...], trace)


def up_two_kernel(
    layer, lone, first_ref, far_ref, second_ref, near_ref, same_ref, other_far_ref, other_same_ref, other_near_ref,
    dense_ref, down_ref, below_ref, wait_ref, kept_ref, other_ref, send_ref, up_ref, back_ref, trace_ref, pairs_ref,
):
    up_ref[...] = kept_ref[...]
    back_ref[...] = other_ref[...]
    trace_ref[...] = down_ref[...]

    @pl.when(lax.axis_index("depth") == layer)
    def _():
        others = (other_far_ref, other_same_ref, other_near_ref)
        totals = three((first_ref, second_ref), far_ref, near_ref, same_ref, others, pairs_ref)
        window = [total.astype(jnp.bfloat16) for total in totals]
        back_ref[...] = window[1]
        below = down_ref[...] if lone else below_ref[...]
        trace_ref[...] = below
        trace = plus(below, applied(window, dense_ref))
        up_ref[...] = trace
        send_ref[...] = trace if lone else plus(wait_ref[...], trace)


def end_kernel(layers, up_ref, returned_ref, out_ref):
    layer = lax.axis_index("depth")
    elsewhere = functools.reduce(jnp.logical_or, [layer == k for k in layers])

    @pl.when(elsewhere)
    def _():
        out_ref[...] = returned_ref[...]

    @pl.when(jnp.logical_not(elsewhere))
    def _():
        out_ref[...] = up_ref[...]


def vmem(count):
    return [pl.BlockSpec(memory_space=pltpu.VMEM)] * count


def local(forcing, blocks, block_rows, block_cols):
    layers, lats = lax.axis_size("depth"), lax.axis_size("lat")
    field = forcing[0]
    _, sources, width = field.shape
    count, parts, size, _ = blocks.shape[1:]
    rows = width // size
    top, split = layers - 1, layers // 2 - 1

    def sent(value, steps, place):
        pairs = [
            (k * lats + j, to_k * lats + place(j))
            for k, to_k in steps
            for j in range(lats)
            if 0 <= place(j) < lats
        ]
        return lax.ppermute(value, AXES, pairs)

    def far(j):
        return j + 1 if j % 2 else j - 1

    def near(j):
        return j - 1 if j % 2 else j + 1

    def same(j):
        return j

    def first(j):
        return j + 2 if j % 4 > 1 else j - 2

    def second(j):
        return j - 2 if j % 4 > 1 else j + 2

    rounds = [(k, k + 1) for k in range(split)] + [(k, k + 2) for k in range(split, top, 2)]
    rounds += [(top, top - 1)] + [(k, k - 2) for k in range(top - 1, 2, -2)] + [(2, 1), (1, 0)]
    wide, narrow = {step: [step] for step in rounds}, {step: [step] for step in rounds}
    if layers == 8:
        narrow |= {step: [(2, 3), (7, 6)] for step in ((2, 3), (7, 6))}
        for shared in ([(5, 7), (4, 2)], [(3, 5), (6, 4)]):
            narrow |= {step: shared for step in shared}
            wide |= {step: shared for step in shared}

    def moved(value, k, to_k, halos=()):
        step = narrow[k, to_k]
        return sent(value, [(k, to_k), *halos], far), sent(value, [*step, *halos], near), sent(value, step, same)

    def moved_two(value, k, to_k):
        outer, inner = wide[k, to_k], narrow[k, to_k]
        return (
            sent(value, outer, first),
            sent(value, outer, far),
            sent(value, outer, second),
            sent(value, inner, near),
            sent(value, inner, same),
        )

    following = sent(field, [(k, k - 1) for k in range(1, layers)], same)

    left_is_far = lax.axis_index("lat") % 2 == 0
    cols = jnp.where(left_is_far, block_cols, 2 * rows - block_cols // rows * rows + block_cols % rows)
    matrix = jax.ShapeDtypeStruct((3 * width, parts * width), jnp.bfloat16)
    dense = pl.pallas_call(
        dense_kernel,
        out_shape=matrix,
        in_specs=[pl.BlockSpec(memory_space=pltpu.SMEM)] * 2 + vmem(1),
        out_specs=pl.BlockSpec(memory_space=pltpu.VMEM),
        scratch_shapes=[pltpu.VMEM((rows, 3 * rows, parts, size, size), jnp.float32)],
        compiler_params=PARAMS,
        name="dense",
    )(block_rows, cols, blocks[0])

    one = jax.ShapeDtypeStruct(field.shape, jnp.bfloat16)
    two = jax.ShapeDtypeStruct((2, *field.shape), jnp.bfloat16)

    def step(kernel, out_shape, layer, *operands, pairs=False):
        return pl.pallas_call(
            functools.partial(kernel, *layer),
            out_shape=out_shape,
            in_specs=vmem(len(operands)),
            out_specs=tuple(vmem(len(out_shape))),
            scratch_shapes=[pltpu.VMEM(two.shape, two.dtype)] if pairs else [],
            compiler_params=PARAMS,
            name=kernel.__name__,
        )(*operands)

    def hold(value, *others):
        return pl.pallas_call(
            hold_kernel,
            out_shape=one,
            in_specs=vmem(1) + [pl.BlockSpec(memory_space=pl.ANY)] * len(others),
            out_specs=pl.BlockSpec(memory_space=pltpu.VMEM),
            compiler_params=PARAMS,
            name="hold",
        )(value, *others)

    ups = [(k + 1, k) for k in range(2, top - 1, 2)]
    downs = [(k, k + 1) for k in range(split + 1, top, 2)]
    given = [*ups, *downs]
    send, down = field, jnp.zeros(field.shape, jnp.bfloat16)
    window = (sent(field, [(0, 0)], far), sent(field, [(0, 0)], near), field)
    for layer in range(split + 1):
        if layer == 1:
            following = hold(following, other_same)
        if layer == split:
            following = hold(following, other_far, other_near)
        send, down = step(down_kernel, (one, one), (layer,), following, *window, dense, down, send)
        if layer == 0:
            [copy] = step(later_kernel, (matrix,), ([k for k, _ in given],), dense, send)
            other_far, other_near, other_same = (sent(copy, given, place) for place in (far, near, same))
        if layer < split:
            window = moved(send, layer, layer + 1, [(k, k) for _, k in downs] if layer == 1 else ())
        if layer == 1:
            field_far, field_near, _ = window
    for layer in range(split + 2, top + 1, 2):
        window = moved_two(send, layer - 2, layer)
        send, down, kept, both = step(
            down_two_kernel, (one, one, one, two), (layer,), *window, other_far, other_same, other_near, dense,
            field_far, field, field_near, following, down, send, pairs=True,
        )
        if layer < top:
            wait, below = sent(kept, [(2, 4), (5, 6)], same), sent(both[1], [(5, 4)], same)
    window = moved(both, top, top - 1)
    send, up, down = step(turn_kernel, (one,) * 3, (top - 1,), *window, dense, wait, down)
    back = jnp.zeros(field.shape, jnp.bfloat16)
    for layer in range(top - 3, 1, -2):
        window = moved_two(send, layer + 2, layer)
        send, up, back, down = step(
            up_two_kernel, (one,) * 4, (layer, layer == 2), *window, other_far, other_same, other_near, dense,
            down, below, wait, up, back, pairs=True,
        )
    returned = sent(back, [(to_k, k) for k, to_k in ups], same)
    [up] = step(up_kernel, (one,), (1,), *moved(send, 2, 1), dense, down, up)
    [up] = step(end_kernel, (one,), ([k for k, _ in ups],), up, returned)
    [up] = step(up_kernel, (one,), (0,), *moved(up, 1, 0), dense, down, up)
    return (down.reshape(forcing.shape), up.reshape(forcing.shape))


def solution(mesh):
    placed = (
        P("depth", None, None, "lat"),
        P("depth", "lat", None, None, None),
        P("depth", "lat"),
        P("depth", "lat"),
    )
    return jax.shard_map(
        local,
        mesh=mesh,
        in_specs=placed,
        out_specs=(P("depth", None, None, "lat"), P("depth", None, None, "lat")),
        check_vma=False,
    )
```

```python
import functools

import jax
import jax.numpy as jnp
from jax import lax
from jax.experimental import pallas as pl
from jax.experimental.pallas import tpu as pltpu
from jax.sharding import PartitionSpec as P

AXES = ("depth", "lat")
PARAMS = pltpu.CompilerParams(vmem_limit_bytes=24 * 2**20)


def dense_kernel(rows_ref, cols_ref, blocks_ref, dense_ref, total_ref):
    count, parts, size, _ = blocks_ref.shape
    rows, slots = total_ref.shape[:2]
    total_ref[...] = jnp.zeros_like(total_ref)
    for b in range(count):
        total_ref[rows_ref[0, b], cols_ref[0, b]] += blocks_ref[b].astype(jnp.float32)
    for r in range(rows):
        for s in range(slots):
            for p in range(parts):
                column = (p * rows + r) * size
                dense_ref[s * size : (s + 1) * size, column : column + size] = (
                    total_ref[r, s, p].T.astype(jnp.bfloat16)
                )


def hold_kernel(field_ref, *refs):
    refs[-1][...] = field_ref[...]


def later_kernel(layers, dense_ref, next_ref, _after, load_ref):
    layer = lax.axis_index("depth")
    depth, width = dense_ref.shape[0], next_ref.shape[2]

    @pl.when(functools.reduce(jnp.logical_or, [layer == k for k in layers]))
    def _():
        load_ref[:depth] = dense_ref[...]
        load_ref[depth:, :width] = next_ref[0]
        load_ref[depth:, width:] = next_ref[1]


def up_kernel(layer, far_ref, near_ref, same_ref, dense_ref, down_ref, kept_ref, up_ref):
    up_ref[...] = kept_ref[...]

    @pl.when(lax.axis_index("depth") == layer)
    def _():
        window = (far_ref[...], same_ref[...], near_ref[...])
        up_ref[...] = plus(down_ref[...], applied(window, dense_ref))


def applied(window, dense_ref):
    sources, width = window[0].shape[1:]
    flat = jnp.concatenate([part.reshape(2 * sources, width) for part in window], axis=1)
    product = jnp.dot(flat, dense_ref[: flat.shape[1]], preferred_element_type=jnp.float32)
    by_real, by_imag = product[:, :width], product[:, width:]
    real = by_real[:sources] - by_imag[sources:]
    imag = by_real[sources:] + by_imag[:sources]
    return jnp.stack([real, imag])


def plus(field, trace):
    return (field.astype(jnp.float32) + trace.astype(jnp.float32)).astype(jnp.bfloat16)


def three(outer, far_ref, near_ref, same_ref, dense_refs, pairs_ref):
    first_ref, second_ref = outer
    place = lax.axis_index("lat") % 4
    first_is_far = (place == 0) | (place == 3)

    @pl.when(first_is_far)
    def _():
        pairs_ref[0] = first_ref[...]
        pairs_ref[1] = second_ref[...]

    @pl.when(jnp.logical_not(first_is_far))
    def _():
        pairs_ref[0] = second_ref[...]
        pairs_ref[1] = first_ref[...]

    far, near, same = far_ref[...], near_ref[...], same_ref[...]
    return (
        applied((same, far, pairs_ref[0]), dense_refs[0]),
        applied((far, same, near), dense_refs[1]),
        applied((pairs_ref[1], near, same), dense_refs[2]),
    )


def down_kernel(layer, next_ref, far_ref, near_ref, same_ref, dense_ref, kept_ref, sent_ref, send_ref, down_ref):
    down_ref[...] = kept_ref[...]
    send_ref[...] = sent_ref[...]

    @pl.when(lax.axis_index("depth") == layer)
    def _():
        window = (far_ref[...], same_ref[...], near_ref[...])
        trace = applied(window, dense_ref).astype(jnp.bfloat16)
        down_ref[...] = trace
        send_ref[...] = plus(next_ref[...], trace)


def down_two_kernel(
    layer, first_ref, far_ref, second_ref, near_ref, same_ref, other_far_ref, other_same_ref, other_near_ref,
    dense_ref, field_ref, next_ref, kept_ref, sent_ref, down_ref, both_ref, *rest,
):
    *more_refs, pairs_ref = rest
    down_ref[...] = kept_ref[...]
    for ref in more_refs[1:]:
        ref[...] = sent_ref[...]

    @pl.when(lax.axis_index("depth") == layer)
    def _():
        others = (other_far_ref, other_same_ref, other_near_ref)
        traces = [
            total.astype(jnp.bfloat16)
            for total in three((first_ref, second_ref), far_ref, near_ref, same_ref, others, pairs_ref)
        ]
        depth, width = dense_ref.shape[0], field_ref.shape[2]
        beside = [
            jnp.stack([ref[depth:, :width], ref[depth:, width:]]) for ref in (other_far_ref, other_near_ref)
        ]
        fields = (beside[0], field_ref[...], beside[1])
        window = [plus(field, trace) for field, trace in zip(fields, traces)]
        trace = applied(window, dense_ref).astype(jnp.bfloat16)
        down_ref[...] = trace
        if more_refs:
            send_ref, wait_ref = more_refs
            send_ref[...] = plus(next_ref[...], trace)
            wait_ref[...] = window[1]
        both_ref[0] = trace
        both_ref[1] = traces[1]


def turn_kernel(layer, far_ref, near_ref, both_ref, dense_ref, wait_ref, kept_ref, send_ref, up_ref, down_ref):
    up_ref[...] = kept_ref[...]
    down_ref[...] = kept_ref[...]

    @pl.when(lax.axis_index("depth") == layer)
    def _():
        down_ref[...] = both_ref[1]
        window = (far_ref[0], both_ref[0], near_ref[0])
        trace = plus(both_ref[1], applied(window, dense_ref))
        up_ref[...] = trace
        send_ref[...] = plus(wait_ref[...], trace)


def up_two_kernel(
    layer, lone, first_ref, far_ref, second_ref, near_ref, same_ref, other_far_ref, other_same_ref, other_near_ref,
    dense_ref, down_ref, below_ref, wait_ref, kept_ref, other_ref, send_ref, up_ref, back_ref, pairs_ref,
):
    up_ref[...] = kept_ref[...]
    back_ref[...] = other_ref[...]

    @pl.when(lax.axis_index("depth") == layer)
    def _():
        others = (other_far_ref, other_same_ref, other_near_ref)
        totals = three((first_ref, second_ref), far_ref, near_ref, same_ref, others, pairs_ref)
        window = [total.astype(jnp.bfloat16) for total in totals]
        back_ref[...] = window[1]
        below = down_ref[...] if lone else below_ref[...]
        trace = plus(below, applied(window, dense_ref))
        up_ref[...] = trace
        send_ref[...] = trace if lone else plus(wait_ref[...], trace)


def chosen_kernel(layers, up_ref, returned_ref, out_ref):
    layer = lax.axis_index("depth")
    out_ref[...] = up_ref[...]

    @pl.when(functools.reduce(jnp.logical_or, [layer == k for k in layers]))
    def _():
        out_ref[...] = returned_ref[...]


def last_kernel(passed, far_ref, near_ref, same_ref, dense_ref, down_ref, below_ref, kept_ref, up_out_ref, down_out_ref):
    layer = lax.axis_index("depth")
    up_out_ref[...] = kept_ref[...]
    down_out_ref[...] = down_ref[...]

    @pl.when(layer == passed)
    def _():
        down_out_ref[...] = below_ref[...]

    @pl.when(layer == 0)
    def _():
        window = (far_ref[...], same_ref[...], near_ref[...])
        up_out_ref[...] = plus(down_ref[...], applied(window, dense_ref))


def vmem(count):
    return [pl.BlockSpec(memory_space=pltpu.VMEM)] * count


def local(forcing, blocks, block_rows, block_cols):
    layers, lats = lax.axis_size("depth"), lax.axis_size("lat")
    field = forcing[0]
    _, sources, width = field.shape
    count, parts, size, _ = blocks.shape[1:]
    rows = width // size
    top, split = layers - 1, layers // 2 - 1

    def sent(value, steps, place):
        pairs = [
            (k * lats + j, to_k * lats + place(j))
            for k, to_k in steps
            for j in range(lats)
            if 0 <= place(j) < lats
        ]
        return lax.ppermute(value, AXES, pairs)

    def far(j):
        return j + 1 if j % 2 else j - 1

    def near(j):
        return j - 1 if j % 2 else j + 1

    def same(j):
        return j

    def first(j):
        return j + 2 if j % 4 > 1 else j - 2

    def second(j):
        return j - 2 if j % 4 > 1 else j + 2

    rounds = [(k, k + 1) for k in range(split)] + [(k, k + 2) for k in range(split, top, 2)]
    rounds += [(top, top - 1)] + [(k, k - 2) for k in range(top - 1, 2, -2)] + [(2, 1), (1, 0)]
    wide, narrow = {step: [step] for step in rounds}, {step: [step] for step in rounds}
    if layers == 8:
        narrow |= {step: [(2, 3), (7, 6)] for step in ((2, 3), (7, 6))}
        for shared in ([(5, 7), (4, 2)], [(3, 5), (6, 4)]):
            narrow |= {step: shared for step in shared}
            wide |= {step: shared for step in shared}

    def moved(value, k, to_k):
        step = narrow[k, to_k]
        return sent(value, [(k, to_k)], far), sent(value, step, near), sent(value, step, same)

    def moved_two(value, k, to_k):
        outer, inner = wide[k, to_k], narrow[k, to_k]
        return (
            sent(value, outer, first),
            sent(value, outer, far),
            sent(value, outer, second),
            sent(value, inner, near),
            sent(value, inner, same),
        )

    following = sent(field, [(k, k - 1) for k in range(1, layers)], same)

    left_is_far = lax.axis_index("lat") % 2 == 0
    cols = jnp.where(left_is_far, block_cols, 2 * rows - block_cols // rows * rows + block_cols % rows)
    matrix = jax.ShapeDtypeStruct((3 * width, parts * width), jnp.bfloat16)
    payload = jax.ShapeDtypeStruct((3 * width + sources, parts * width), jnp.bfloat16)
    dense = pl.pallas_call(
        dense_kernel,
        out_shape=matrix,
        in_specs=[pl.BlockSpec(memory_space=pltpu.SMEM)] * 2 + vmem(1),
        out_specs=pl.BlockSpec(memory_space=pltpu.VMEM),
        scratch_shapes=[pltpu.VMEM((rows, 3 * rows, parts, size, size), jnp.float32)],
        compiler_params=PARAMS,
        name="dense",
    )(block_rows, cols, blocks[0])

    one = jax.ShapeDtypeStruct(field.shape, jnp.bfloat16)
    two = jax.ShapeDtypeStruct((2, *field.shape), jnp.bfloat16)

    def step(kernel, out_shape, layer, *operands, pairs=False):
        return pl.pallas_call(
            functools.partial(kernel, *layer),
            out_shape=out_shape,
            in_specs=vmem(len(operands)),
            out_specs=tuple(vmem(len(out_shape))),
            scratch_shapes=[pltpu.VMEM(two.shape, two.dtype)] if pairs else [],
            compiler_params=PARAMS,
            name=kernel.__name__,
        )(*operands)

    def hold(value, *others):
        return pl.pallas_call(
            hold_kernel,
            out_shape=one,
            in_specs=vmem(1) + [pl.BlockSpec(memory_space=pl.ANY)] * len(others),
            out_specs=pl.BlockSpec(memory_space=pltpu.VMEM),
            compiler_params=PARAMS,
            name="hold",
        )(value, *others)

    ups = [(k + 1, k) for k in range(2, top - 1, 2)]
    downs = [(k, k + 1) for k in range(split + 1, top, 2)]
    given = [*ups, *downs]
    send, down = field, jnp.zeros(field.shape, jnp.bfloat16)
    window = (sent(field, [(0, 0)], far), sent(field, [(0, 0)], near), field)
    for layer in range(split + 1):
        if layer == 1:
            following = hold(following, other_same)
        if layer == split:
            following = hold(following, other_far, other_near)
        send, down = step(down_kernel, (one, one), (layer,), following, *window, dense, down, send)
        if layer < split:
            window = moved(send, layer, layer + 1)
        if layer == 0:
            [load] = step(later_kernel, (payload,), ([k for k, _ in given],), dense, following, send)
            other_far, other_near, other_same = (sent(load, given, place) for place in (far, near, same))
    for layer in range(split + 2, top + 1, 2):
        window = moved_two(send, layer - 2, layer)
        down, both, *more = step(
            down_two_kernel, (one, two, one, one)[: 4 if layer < top else 2], (layer,), *window,
            other_far, other_same, other_near, dense, field, following, down, send, pairs=True,
        )
        if layer < top:
            send, kept = more
            wait, below = sent(kept, [(2, 4), (5, 6)], same), sent(both[1], [(5, 4)], same)
    window = moved(both, top, top - 1)
    send, up, down = step(turn_kernel, (one,) * 3, (top - 1,), *window, dense, wait, down)
    back = jnp.zeros(field.shape, jnp.bfloat16)
    for layer in range(top - 3, 1, -2):
        window = moved_two(send, layer + 2, layer)
        send, up, back = step(
            up_two_kernel, (one,) * 3, (layer, layer == 2), *window, other_far, other_same, other_near, dense,
            down, below, wait, up, back, pairs=True,
        )
    returned = sent(back, [(to_k, k) for k, to_k in ups], same)
    [up] = step(up_kernel, (one,), (1,), *moved(send, 2, 1), dense, down, up)
    [up] = step(chosen_kernel, (one,), ([k for k, _ in ups],), up, returned)
    up, down = step(last_kernel, (one, one), (split + 1,), *moved(up, 1, 0), dense, down, below, up)
    return (down.reshape(forcing.shape), up.reshape(forcing.shape))


def solution(mesh):
    placed = (
        P("depth", None, None, "lat"),
        P("depth", "lat", None, None, None),
        P("depth", "lat"),
        P("depth", "lat"),
    )
    return jax.shard_map(
        local,
        mesh=mesh,
        in_specs=placed,
        out_specs=(P("depth", None, None, "lat"), P("depth", None, None, "lat")),
        check_vma=False,
    )
```

```python
import functools

import jax
import jax.numpy as jnp
from jax import lax
from jax.experimental import pallas as pl
from jax.experimental.pallas import tpu as pltpu
from jax.sharding import PartitionSpec as P

AXES = ("depth", "lat")
PARAMS = pltpu.CompilerParams(vmem_limit_bytes=24 * 2**20)


def dense_kernel(rows_ref, cols_ref, blocks_ref, dense_ref, total_ref):
    count, parts, size, _ = blocks_ref.shape
    rows, slots = total_ref.shape[:2]
    total_ref[...] = jnp.zeros_like(total_ref)
    for b in range(count):
        total_ref[rows_ref[0, b], cols_ref[0, b]] += blocks_ref[b].astype(jnp.float32)
    for r in range(rows):
        for s in range(slots):
            for p in range(parts):
                column = (p * rows + r) * size
                dense_ref[s * size : (s + 1) * size, column : column + size] = (
                    total_ref[r, s, p].T.astype(jnp.bfloat16)
                )


def hold_kernel(field_ref, *refs):
    refs[-1][...] = field_ref[...]


def later_kernel(layers, dense_ref, next_ref, _after, load_ref):
    layer = lax.axis_index("depth")
    depth, width = dense_ref.shape[0], next_ref.shape[2]

    @pl.when(functools.reduce(jnp.logical_or, [layer == k for k in layers]))
    def _():
        load_ref[:depth] = dense_ref[...]
        load_ref[depth:, :width] = next_ref[0]
        load_ref[depth:, width:] = next_ref[1]


def up_kernel(layer, far_ref, near_ref, same_ref, dense_ref, down_ref, kept_ref, up_ref):
    up_ref[...] = kept_ref[...]

    @pl.when(lax.axis_index("depth") == layer)
    def _():
        window = (far_ref[...], same_ref[...], near_ref[...])
        up_ref[...] = plus(down_ref[...], applied(window, dense_ref))


def applied(window, dense_ref):
    sources, width = window[0].shape[1:]
    flat = jnp.concatenate([part.reshape(2 * sources, width) for part in window], axis=1)
    product = jnp.dot(flat, dense_ref[: flat.shape[1]], preferred_element_type=jnp.float32)
    by_real, by_imag = product[:, :width], product[:, width:]
    real = by_real[:sources] - by_imag[sources:]
    imag = by_real[sources:] + by_imag[:sources]
    return jnp.stack([real, imag])


def plus(field, trace):
    return (field.astype(jnp.float32) + trace.astype(jnp.float32)).astype(jnp.bfloat16)


def three(outer, far_ref, near_ref, same_ref, dense_refs, pairs_ref):
    first_ref, second_ref = outer
    place = lax.axis_index("lat") % 4
    first_is_far = (place == 0) | (place == 3)

    @pl.when(first_is_far)
    def _():
        pairs_ref[0] = first_ref[...]
        pairs_ref[1] = second_ref[...]

    @pl.when(jnp.logical_not(first_is_far))
    def _():
        pairs_ref[0] = second_ref[...]
        pairs_ref[1] = first_ref[...]

    far, near, same = far_ref[...], near_ref[...], same_ref[...]
    return (
        applied((same, far, pairs_ref[0]), dense_refs[0]),
        applied((far, same, near), dense_refs[1]),
        applied((pairs_ref[1], near, same), dense_refs[2]),
    )


def down_kernel(layer, shift, next_ref, *refs):
    *window_refs, dense_ref, kept_ref, sent_ref, send_ref, down_ref = refs
    far_ref, near_ref, same_ref = window_refs[-shift:] + window_refs[:-shift] if shift else window_refs
    down_ref[...] = kept_ref[...]
    send_ref[...] = sent_ref[...]

    @pl.when(lax.axis_index("depth") == layer)
    def _():
        window = (far_ref[...], same_ref[...], near_ref[...])
        trace = applied(window, dense_ref).astype(jnp.bfloat16)
        down_ref[...] = trace
        send_ref[...] = plus(next_ref[...], trace)


def down_two_kernel(
    layer, first_ref, far_ref, second_ref, near_ref, same_ref, other_far_ref, other_same_ref, other_near_ref,
    dense_ref, field_ref, next_ref, kept_ref, sent_ref, down_ref, both_ref, *rest,
):
    *more_refs, pairs_ref = rest
    down_ref[...] = kept_ref[...]
    for ref in more_refs[1:]:
        ref[...] = sent_ref[...]

    @pl.when(lax.axis_index("depth") == layer)
    def _():
        others = (other_far_ref, other_same_ref, other_near_ref)
        traces = [
            total.astype(jnp.bfloat16)
            for total in three((first_ref, second_ref), far_ref, near_ref, same_ref, others, pairs_ref)
        ]
        depth, width = dense_ref.shape[0], field_ref.shape[2]
        beside = [
            jnp.stack([ref[depth:, :width], ref[depth:, width:]]) for ref in (other_far_ref, other_near_ref)
        ]
        fields = (beside[0], field_ref[...], beside[1])
        window = [plus(field, trace) for field, trace in zip(fields, traces)]
        trace = applied(window, dense_ref).astype(jnp.bfloat16)
        down_ref[...] = trace
        if more_refs:
            send_ref, wait_ref = more_refs
            send_ref[...] = plus(next_ref[...], trace)
            wait_ref[...] = window[1]
        both_ref[0] = trace
        both_ref[1] = traces[1]


def turn_kernel(layer, far_ref, near_ref, both_ref, dense_ref, wait_ref, kept_ref, send_ref, up_ref, down_ref):
    up_ref[...] = kept_ref[...]
    down_ref[...] = kept_ref[...]

    @pl.when(lax.axis_index("depth") == layer)
    def _():
        down_ref[...] = both_ref[1]
        window = (far_ref[0], both_ref[0], near_ref[0])
        trace = plus(both_ref[1], applied(window, dense_ref))
        up_ref[...] = trace
        send_ref[...] = plus(wait_ref[...], trace)


def up_two_kernel(
    layer, lone, first_ref, far_ref, second_ref, near_ref, same_ref, other_far_ref, other_same_ref, other_near_ref,
    dense_ref, down_ref, below_ref, wait_ref, kept_ref, other_ref, send_ref, up_ref, back_ref, pairs_ref,
):
    up_ref[...] = kept_ref[...]
    back_ref[...] = other_ref[...]

    @pl.when(lax.axis_index("depth") == layer)
    def _():
        others = (other_far_ref, other_same_ref, other_near_ref)
        totals = three((first_ref, second_ref), far_ref, near_ref, same_ref, others, pairs_ref)
        window = [total.astype(jnp.bfloat16) for total in totals]
        back_ref[...] = window[1]
        below = down_ref[...] if lone else below_ref[...]
        trace = plus(below, applied(window, dense_ref))
        up_ref[...] = trace
        send_ref[...] = trace if lone else plus(wait_ref[...], trace)


def chosen_kernel(layers, up_ref, returned_ref, out_ref):
    layer = lax.axis_index("depth")
    out_ref[...] = up_ref[...]

    @pl.when(functools.reduce(jnp.logical_or, [layer == k for k in layers]))
    def _():
        out_ref[...] = returned_ref[...]


def last_kernel(passed, far_ref, near_ref, same_ref, dense_ref, down_ref, below_ref, kept_ref, up_out_ref, down_out_ref):
    layer = lax.axis_index("depth")
    up_out_ref[...] = kept_ref[...]
    down_out_ref[...] = down_ref[...]

    @pl.when(layer == passed)
    def _():
        down_out_ref[...] = below_ref[...]

    @pl.when(layer == 0)
    def _():
        window = (far_ref[...], same_ref[...], near_ref[...])
        up_out_ref[...] = plus(down_ref[...], applied(window, dense_ref))


def vmem(count):
    return [pl.BlockSpec(memory_space=pltpu.VMEM)] * count


def local(forcing, blocks, block_rows, block_cols):
    layers, lats = lax.axis_size("depth"), lax.axis_size("lat")
    field = forcing[0]
    _, sources, width = field.shape
    count, parts, size, _ = blocks.shape[1:]
    rows = width // size
    top, split = layers - 1, layers // 2 - 1

    def sent(value, steps, place):
        pairs = [
            (k * lats + j, to_k * lats + place(j))
            for k, to_k in steps
            for j in range(lats)
            if 0 <= place(j) < lats
        ]
        return lax.ppermute(value, AXES, pairs)

    def far(j):
        return j + 1 if j % 2 else j - 1

    def near(j):
        return j - 1 if j % 2 else j + 1

    def same(j):
        return j

    def first(j):
        return j + 2 if j % 4 > 1 else j - 2

    def second(j):
        return j - 2 if j % 4 > 1 else j + 2

    rounds = [(k, k + 1) for k in range(split)] + [(k, k + 2) for k in range(split, top, 2)]
    rounds += [(top, top - 1)] + [(k, k - 2) for k in range(top - 1, 2, -2)] + [(2, 1), (1, 0)]
    wide, narrow = {step: [step] for step in rounds}, {step: [step] for step in rounds}
    if layers == 8:
        narrow |= {step: [(2, 3), (7, 6)] for step in ((2, 3), (7, 6))}
        for shared in ([(5, 7), (4, 2)], [(3, 5), (6, 4)]):
            narrow |= {step: shared for step in shared}
            wide |= {step: shared for step in shared}

    def moved(value, k, to_k):
        step = narrow[k, to_k]
        return sent(value, [(k, to_k)], far), sent(value, step, near), sent(value, step, same)

    def moved_two(value, k, to_k):
        outer, inner = wide[k, to_k], narrow[k, to_k]
        return (
            sent(value, outer, first),
            sent(value, outer, far),
            sent(value, outer, second),
            sent(value, inner, near),
            sent(value, inner, same),
        )

    following = sent(field, [(k, k - 1) for k in range(1, layers)], same)

    left_is_far = lax.axis_index("lat") % 2 == 0
    cols = jnp.where(left_is_far, block_cols, 2 * rows - block_cols // rows * rows + block_cols % rows)
    matrix = jax.ShapeDtypeStruct((3 * width, parts * width), jnp.bfloat16)
    payload = jax.ShapeDtypeStruct((3 * width + sources, parts * width), jnp.bfloat16)
    dense = pl.pallas_call(
        dense_kernel,
        out_shape=matrix,
        in_specs=[pl.BlockSpec(memory_space=pltpu.SMEM)] * 2 + vmem(1),
        out_specs=pl.BlockSpec(memory_space=pltpu.VMEM),
        scratch_shapes=[pltpu.VMEM((rows, 3 * rows, parts, size, size), jnp.float32)],
        compiler_params=PARAMS,
        name="dense",
    )(block_rows, cols, blocks[0])

    one = jax.ShapeDtypeStruct(field.shape, jnp.bfloat16)
    two = jax.ShapeDtypeStruct((2, *field.shape), jnp.bfloat16)

    def step(kernel, out_shape, layer, *operands, pairs=False):
        return pl.pallas_call(
            functools.partial(kernel, *layer),
            out_shape=out_shape,
            in_specs=vmem(len(operands)),
            out_specs=tuple(vmem(len(out_shape))),
            scratch_shapes=[pltpu.VMEM(two.shape, two.dtype)] if pairs else [],
            compiler_params=PARAMS,
            name=kernel.__name__,
        )(*operands)

    def hold(value, *others):
        return pl.pallas_call(
            hold_kernel,
            out_shape=one,
            in_specs=vmem(1) + [pl.BlockSpec(memory_space=pl.ANY)] * len(others),
            out_specs=pl.BlockSpec(memory_space=pltpu.VMEM),
            compiler_params=PARAMS,
            name="hold",
        )(value, *others)

    ups = [(k + 1, k) for k in range(2, top - 1, 2)]
    downs = [(k, k + 1) for k in range(split + 1, top, 2)]
    given = [*ups, *downs]
    send, down = field, jnp.zeros(field.shape, jnp.bfloat16)
    window = (sent(field, [(0, 0)], far), sent(field, [(0, 0)], near), field)
    for layer in range(split + 1):
        if layer == 1:
            following = hold(following, other_same)
        if layer == split:
            following = hold(following, other_near)
        shift = 1 if layer == 2 else 0
        parts = [*window[shift:], *window[:shift]]
        send, down = step(down_kernel, (one, one), (layer, shift), following, *parts, dense, down, send)
        if layer < split:
            window = moved(send, layer, layer + 1)
        if layer == 0:
            [load] = step(later_kernel, (payload,), ([k for k, _ in given],), dense, following, send)
            other_far, other_near, other_same = (sent(load, given, place) for place in (far, near, same))
    for layer in range(split + 2, top + 1, 2):
        following = hold(following, other_far) if layer < top else following
        window = moved_two(send, layer - 2, layer)
        down, both, *more = step(
            down_two_kernel, (one, two, one, one)[: 4 if layer < top else 2], (layer,), *window,
            other_far, other_same, other_near, dense, field, following, down, send, pairs=True,
        )
        if layer < top:
            send, kept = more
            wait, below = sent(kept, [(2, 4), (5, 6)], same), sent(both[1], [(5, 4)], same)
    window = moved(both, top, top - 1)
    send, up, down = step(turn_kernel, (one,) * 3, (top - 1,), *window, dense, wait, down)
    back = jnp.zeros(field.shape, jnp.bfloat16)
    for layer in range(top - 3, 1, -2):
        window = moved_two(send, layer + 2, layer)
        send, up, back = step(
            up_two_kernel, (one,) * 3, (layer, layer == 2), *window, other_far, other_same, other_near, dense,
            down, below, wait, up, back, pairs=True,
        )
    returned = sent(back, [(to_k, k) for k, to_k in ups], same)
    [up] = step(up_kernel, (one,), (1,), *moved(send, 2, 1), dense, down, up)
    [up] = step(chosen_kernel, (one,), ([k for k, _ in ups],), up, returned)
    up, down = step(last_kernel, (one, one), (split + 1,), *moved(up, 1, 0), dense, down, below, up)
    return (down.reshape(forcing.shape), up.reshape(forcing.shape))


def solution(mesh):
    placed = (
        P("depth", None, None, "lat"),
        P("depth", "lat", None, None, None),
        P("depth", "lat"),
        P("depth", "lat"),
    )
    return jax.shard_map(
        local,
        mesh=mesh,
        in_specs=placed,
        out_specs=(P("depth", None, None, "lat"), P("depth", None, None, "lat")),
        check_vma=False,
    )
```

```python
import functools

import jax
import jax.numpy as jnp
from jax import lax
from jax.experimental import pallas as pl
from jax.experimental.pallas import tpu as pltpu
from jax.sharding import PartitionSpec as P

AXES = ("depth", "lat")
PARAMS = pltpu.CompilerParams(vmem_limit_bytes=24 * 2**20)


def dense_kernel(rows_ref, cols_ref, blocks_ref, dense_ref, total_ref):
    count, parts, size, _ = blocks_ref.shape
    rows, slots = total_ref.shape[:2]
    total_ref[...] = jnp.zeros_like(total_ref)
    for b in range(count):
        total_ref[rows_ref[0, b], cols_ref[0, b]] += blocks_ref[b].astype(jnp.float32)
    for r in range(rows):
        for s in range(slots):
            for p in range(parts):
                column = (p * rows + r) * size
                dense_ref[s * size : (s + 1) * size, column : column + size] = (
                    total_ref[r, s, p].T.astype(jnp.bfloat16)
                )


def hold_kernel(field_ref, *refs):
    refs[-1][...] = field_ref[...]


def later_kernel(layers, dense_ref, next_ref, _after, load_ref):
    layer = lax.axis_index("depth")
    depth, width = dense_ref.shape[0], next_ref.shape[2]

    @pl.when(functools.reduce(jnp.logical_or, [layer == k for k in layers]))
    def _():
        load_ref[:depth] = dense_ref[...]
        load_ref[depth:, :width] = next_ref[0]
        load_ref[depth:, width:] = next_ref[1]


def up_kernel(layer, far_ref, near_ref, same_ref, dense_ref, down_ref, kept_ref, up_ref):
    up_ref[...] = kept_ref[...]

    @pl.when(lax.axis_index("depth") == layer)
    def _():
        window = (far_ref[...], same_ref[...], near_ref[...])
        up_ref[...] = plus(down_ref[...], applied(window, dense_ref))


def applied(window, dense_ref):
    sources, width = window[0].shape[1:]
    flat = jnp.concatenate([part.reshape(2 * sources, width) for part in window], axis=1)
    product = jnp.dot(flat, dense_ref[: flat.shape[1]], preferred_element_type=jnp.float32)
    by_real, by_imag = product[:, :width], product[:, width:]
    real = by_real[:sources] - by_imag[sources:]
    imag = by_real[sources:] + by_imag[:sources]
    return jnp.stack([real, imag])


def plus(field, trace):
    return (field.astype(jnp.float32) + trace.astype(jnp.float32)).astype(jnp.bfloat16)


def three(outer, far_ref, near_ref, same_ref, dense_refs, pairs_ref):
    first_ref, second_ref = outer
    place = lax.axis_index("lat") % 4
    first_is_far = (place == 0) | (place == 3)

    @pl.when(first_is_far)
    def _():
        pairs_ref[0] = first_ref[...]
        pairs_ref[1] = second_ref[...]

    @pl.when(jnp.logical_not(first_is_far))
    def _():
        pairs_ref[0] = second_ref[...]
        pairs_ref[1] = first_ref[...]

    far, near, same = far_ref[...], near_ref[...], same_ref[...]
    return (
        applied((same, far, pairs_ref[0]), dense_refs[0]),
        applied((far, same, near), dense_refs[1]),
        applied((pairs_ref[1], near, same), dense_refs[2]),
    )


def down_kernel(layer, shift, next_ref, *refs):
    *window_refs, dense_ref, kept_ref, sent_ref, send_ref, down_ref = refs
    far_ref, near_ref, same_ref = window_refs[-shift:] + window_refs[:-shift] if shift else window_refs
    down_ref[...] = kept_ref[...]
    send_ref[...] = sent_ref[...]

    @pl.when(lax.axis_index("depth") == layer)
    def _():
        window = (far_ref[...], same_ref[...], near_ref[...])
        trace = applied(window, dense_ref).astype(jnp.bfloat16)
        down_ref[...] = trace
        send_ref[...] = plus(next_ref[...], trace)


def down_two_kernel(
    layer, first_ref, far_ref, second_ref, near_ref, same_ref, other_far_ref, other_same_ref, other_near_ref,
    dense_ref, field_ref, next_ref, kept_ref, sent_ref, passed_ref, send_ref, down_ref, wait_ref, mid_ref, pairs_ref,
):
    down_ref[...] = kept_ref[...]
    wait_ref[...] = sent_ref[...]
    mid_ref[...] = passed_ref[...]

    @pl.when(lax.axis_index("depth") == layer)
    def _():
        others = (other_far_ref, other_same_ref, other_near_ref)
        traces = [
            total.astype(jnp.bfloat16)
            for total in three((first_ref, second_ref), far_ref, near_ref, same_ref, others, pairs_ref)
        ]
        depth, width = dense_ref.shape[0], field_ref.shape[2]
        beside = [
            jnp.stack([ref[depth:, :width], ref[depth:, width:]]) for ref in (other_far_ref, other_near_ref)
        ]
        fields = (beside[0], field_ref[...], beside[1])
        window = [plus(field, trace) for field, trace in zip(fields, traces)]
        trace = applied(window, dense_ref).astype(jnp.bfloat16)
        down_ref[...] = trace
        send_ref[...] = plus(next_ref[...], trace)
        wait_ref[...] = window[1]
        mid_ref[...] = traces[1]


def turn_kernel(layer, far_ref, near_ref, same_ref, dense_ref, wait_ref, kept_ref, send_ref, down_ref):
    down_ref[...] = kept_ref[...]

    @pl.when(lax.axis_index("depth") == layer)
    def _():
        window = (far_ref[...], same_ref[...], near_ref[...])
        trace = applied(window, dense_ref).astype(jnp.bfloat16)
        down_ref[...] = trace
        send_ref[...] = plus(wait_ref[...], trace)


def up_two_kernel(
    layer, lone, first_ref, far_ref, second_ref, near_ref, same_ref, other_far_ref, other_same_ref, other_near_ref,
    dense_ref, down_ref, below_ref, wait_ref, kept_ref, other_ref, send_ref, up_ref, back_ref, pairs_ref,
):
    up_ref[...] = kept_ref[...]
    back_ref[...] = other_ref[...]

    @pl.when(lax.axis_index("depth") == layer)
    def _():
        others = (other_far_ref, other_same_ref, other_near_ref)
        totals = three((first_ref, second_ref), far_ref, near_ref, same_ref, others, pairs_ref)
        window = [total.astype(jnp.bfloat16) for total in totals]
        back_ref[...] = window[1]
        below = down_ref[...] if lone else below_ref[...]
        trace = plus(below, applied(window, dense_ref))
        up_ref[...] = trace
        send_ref[...] = trace if lone else plus(wait_ref[...], trace)


def last_kernel(
    passed, returned, far_ref, near_ref, same_ref, dense_ref, down_ref, below_ref, kept_ref, back_ref, up_out_ref, down_out_ref
):
    layer = lax.axis_index("depth")
    up_out_ref[...] = kept_ref[...]
    down_out_ref[...] = down_ref[...]

    @pl.when(functools.reduce(jnp.logical_or, [layer == k for k in passed]))
    def _():
        down_out_ref[...] = below_ref[...]

    @pl.when(functools.reduce(jnp.logical_or, [layer == k for k in returned]))
    def _():
        up_out_ref[...] = back_ref[...]

    @pl.when(layer == 0)
    def _():
        window = (far_ref[...], same_ref[...], near_ref[...])
        up_out_ref[...] = plus(down_ref[...], applied(window, dense_ref))


def vmem(count):
    return [pl.BlockSpec(memory_space=pltpu.VMEM)] * count


def local(forcing, blocks, block_rows, block_cols):
    layers, lats = lax.axis_size("depth"), lax.axis_size("lat")
    field = forcing[0]
    _, sources, width = field.shape
    count, parts, size, _ = blocks.shape[1:]
    rows = width // size
    top, split = layers - 1, layers // 2 - 2

    def sent(value, steps, place):
        pairs = [
            (k * lats + j, to_k * lats + place(j))
            for k, to_k in steps
            for j in range(lats)
            if 0 <= place(j) < lats
        ]
        return lax.ppermute(value, AXES, pairs)

    def far(j):
        return j + 1 if j % 2 else j - 1

    def near(j):
        return j - 1 if j % 2 else j + 1

    def same(j):
        return j

    def first(j):
        return j + 2 if j % 4 > 1 else j - 2

    def second(j):
        return j - 2 if j % 4 > 1 else j + 2

    rounds = [(k, k + 1) for k in range(split)] + [(k, k + 2) for k in range(split, top - 1, 2)]
    rounds += [(top - 1, top)] + [(k, k - 2) for k in range(top, 1, -2)] + [(1, 0)]
    wide, narrow = {step: [step] for step in rounds}, {step: [step] for step in rounds}
    if layers == 8:
        narrow |= {step: [(0, 1), (6, 7)] for step in ((0, 1), (6, 7))}
        for shared in ([(2, 4), (7, 5)], [(4, 6), (3, 1)]):
            narrow |= {step: shared for step in shared}
            wide |= {step: shared for step in shared}

    def moved(value, k, to_k):
        step = narrow[k, to_k]
        return sent(value, [(k, to_k)], far), sent(value, step, near), sent(value, step, same)

    def moved_two(value, k, to_k):
        outer, inner = wide[k, to_k], narrow[k, to_k]
        return (
            sent(value, outer, first),
            sent(value, outer, far),
            sent(value, outer, second),
            sent(value, inner, near),
            sent(value, inner, same),
        )

    following = sent(field, [(k, k - 1) for k in range(1, layers)], same)

    left_is_far = lax.axis_index("lat") % 2 == 0
    cols = jnp.where(left_is_far, block_cols, 2 * rows - block_cols // rows * rows + block_cols % rows)
    matrix = jax.ShapeDtypeStruct((3 * width, parts * width), jnp.bfloat16)
    payload = jax.ShapeDtypeStruct((3 * width + sources, parts * width), jnp.bfloat16)
    dense = pl.pallas_call(
        dense_kernel,
        out_shape=matrix,
        in_specs=[pl.BlockSpec(memory_space=pltpu.SMEM)] * 2 + vmem(1),
        out_specs=pl.BlockSpec(memory_space=pltpu.VMEM),
        scratch_shapes=[pltpu.VMEM((rows, 3 * rows, parts, size, size), jnp.float32)],
        compiler_params=PARAMS,
        name="dense",
    )(block_rows, cols, blocks[0])

    one = jax.ShapeDtypeStruct(field.shape, jnp.bfloat16)
    two = jax.ShapeDtypeStruct((2, *field.shape), jnp.bfloat16)

    def step(kernel, out_shape, layer, *operands, pairs=False):
        return pl.pallas_call(
            functools.partial(kernel, *layer),
            out_shape=out_shape,
            in_specs=vmem(len(operands)),
            out_specs=tuple(vmem(len(out_shape))),
            scratch_shapes=[pltpu.VMEM(two.shape, two.dtype)] if pairs else [],
            compiler_params=PARAMS,
            name=kernel.__name__,
        )(*operands)

    def hold(value, *others):
        return pl.pallas_call(
            hold_kernel,
            out_shape=one,
            in_specs=vmem(1) + [pl.BlockSpec(memory_space=pl.ANY)] * len(others),
            out_specs=pl.BlockSpec(memory_space=pltpu.VMEM),
            compiler_params=PARAMS,
            name="hold",
        )(value, *others)

    ups = [(k + 1, k) for k in range(1, top, 2)]
    downs = [(k, k + 1) for k in range(split + 1, top, 2)]
    given = [*ups, *downs]
    send, down = field, jnp.zeros(field.shape, jnp.bfloat16)
    window = (sent(field, [(0, 0)], far), sent(field, [(0, 0)], near), field)
    for layer in range(split + 1):
        if layer == 1:
            following = hold(following, other_same)
        if layer == 2:
            following = hold(following, other_near)
        shift = 1 if layer == 2 else 0
        parts = [*window[shift:], *window[:shift]]
        send, down = step(down_kernel, (one, one), (layer, shift), following, *parts, dense, down, send)
        if layer < split:
            window = moved(send, layer, layer + 1)
        if layer == 0:
            [load] = step(later_kernel, (payload,), ([k for k, _ in given],), dense, following, send)
            other_far, other_near, other_same = (sent(load, given, place) for place in (far, near, same))
    wait, mid = send, jnp.zeros(field.shape, jnp.bfloat16)
    for layer in range(split + 2, top, 2):
        following = hold(following, other_far) if layer == split + 2 else following
        window = moved_two(send, layer - 2, layer)
        send, down, wait, mid = step(
            down_two_kernel, (one,) * 4, (layer,), *window, other_far, other_same, other_near, dense,
            field, following, down, wait, mid, pairs=True,
        )
    window = moved(send, top - 1, top)
    wait = sent(wait, [(1, 3), (4, 5), (6, 7)], same)
    below = sent(mid, [(4, 3), (6, 5)], same)
    send, down = step(turn_kernel, (one, one), (top,), *window, dense, wait, down)
    up, back = down, jnp.zeros(field.shape, jnp.bfloat16)
    for layer in range(top - 2, 0, -2):
        window = moved_two(send, layer + 2, layer)
        send, up, back = step(
            up_two_kernel, (one,) * 3, (layer, layer == 1), *window, other_far, other_same, other_near, dense,
            down, below, wait, up, back, pairs=True,
        )
    window = moved(send, 1, 0)
    back = sent(back, [(to_k, k) for k, to_k in ups], same)
    up, down = step(last_kernel, (one, one), ([3, 5], [k for k, _ in ups]), *window, dense, down, below, up, back)
    return (down.reshape(forcing.shape), up.reshape(forcing.shape))


def solution(mesh):
    placed = (
        P("depth", None, None, "lat"),
        P("depth", "lat", None, None, None),
        P("depth", "lat"),
        P("depth", "lat"),
    )
    return jax.shard_map(
        local,
        mesh=mesh,
        in_specs=placed,
        out_specs=(P("depth", None, None, "lat"), P("depth", None, None, "lat")),
        check_vma=False,
    )
```

```python
import functools

import jax
import jax.numpy as jnp
from jax import lax
from jax.experimental import pallas as pl
from jax.experimental.pallas import tpu as pltpu
from jax.sharding import PartitionSpec as P

AXES = ("depth", "lat")
PARAMS = pltpu.CompilerParams(vmem_limit_bytes=24 * 2**20)


def dense_kernel(rows_ref, cols_ref, blocks_ref, dense_ref, total_ref):
    count, parts, size, _ = blocks_ref.shape
    rows, slots = total_ref.shape[:2]
    total_ref[...] = jnp.zeros_like(total_ref)
    for b in range(count):
        total_ref[rows_ref[0, b], cols_ref[0, b]] += blocks_ref[b].astype(jnp.float32)
    for r in range(rows):
        for s in range(slots):
            for p in range(parts):
                column = (p * rows + r) * size
                dense_ref[s * size : (s + 1) * size, column : column + size] = (
                    total_ref[r, s, p].T.astype(jnp.bfloat16)
                )


def hold_kernel(field_ref, *refs):
    refs[-1][...] = field_ref[...]


def later_kernel(layers, dense_ref, next_ref, _after, load_ref):
    layer = lax.axis_index("depth")
    depth, width = dense_ref.shape[0], next_ref.shape[2]

    @pl.when(functools.reduce(jnp.logical_or, [layer == k for k in layers]))
    def _():
        load_ref[:depth] = dense_ref[...]
        load_ref[depth:, :width] = next_ref[0]
        load_ref[depth:, width:] = next_ref[1]


def up_kernel(layer, far_ref, near_ref, same_ref, dense_ref, down_ref, kept_ref, up_ref):
    up_ref[...] = kept_ref[...]

    @pl.when(lax.axis_index("depth") == layer)
    def _():
        window = (far_ref[...], same_ref[...], near_ref[...])
        up_ref[...] = plus(down_ref[...], applied(window, dense_ref))


def applied(window, dense_ref):
    sources, width = window[0].shape[1:]
    flat = jnp.concatenate([part.reshape(2 * sources, width) for part in window], axis=1)
    product = jnp.dot(flat, dense_ref[: flat.shape[1]], preferred_element_type=jnp.float32)
    by_real, by_imag = product[:, :width], product[:, width:]
    real = by_real[:sources] - by_imag[sources:]
    imag = by_real[sources:] + by_imag[:sources]
    return jnp.stack([real, imag])


def plus(field, trace):
    return (field.astype(jnp.float32) + trace.astype(jnp.float32)).astype(jnp.bfloat16)


def three(outer, far_ref, near_ref, same_ref, dense_refs, pairs_ref):
    first_ref, second_ref = outer
    place = lax.axis_index("lat") % 4
    first_is_far = (place == 0) | (place == 3)

    @pl.when(first_is_far)
    def _():
        pairs_ref[0] = first_ref[...]
        pairs_ref[1] = second_ref[...]

    @pl.when(jnp.logical_not(first_is_far))
    def _():
        pairs_ref[0] = second_ref[...]
        pairs_ref[1] = first_ref[...]

    far, near, same = far_ref[...], near_ref[...], same_ref[...]
    return (
        applied((same, far, pairs_ref[0]), dense_refs[0]),
        applied((far, same, near), dense_refs[1]),
        applied((pairs_ref[1], near, same), dense_refs[2]),
    )


def down_kernel(layer, shift, next_ref, *refs):
    *window_refs, dense_ref, kept_ref, sent_ref, send_ref, down_ref = refs
    far_ref, near_ref, same_ref = window_refs[-shift:] + window_refs[:-shift] if shift else window_refs
    down_ref[...] = kept_ref[...]
    send_ref[...] = sent_ref[...]

    @pl.when(lax.axis_index("depth") == layer)
    def _():
        window = (far_ref[...], same_ref[...], near_ref[...])
        trace = applied(window, dense_ref).astype(jnp.bfloat16)
        down_ref[...] = trace
        send_ref[...] = plus(next_ref[...], trace)


def down_two_kernel(
    layer, first_ref, far_ref, second_ref, near_ref, same_ref, other_far_ref, other_same_ref, other_near_ref,
    dense_ref, field_ref, next_ref, kept_ref, sent_ref, passed_ref, down_ref, mid_ref, *rest,
):
    *more_refs, pairs_ref = rest
    down_ref[...] = kept_ref[...]
    mid_ref[...] = passed_ref[...]
    for ref in more_refs[1:]:
        ref[...] = sent_ref[...]

    @pl.when(lax.axis_index("depth") == layer)
    def _():
        others = (other_far_ref, other_same_ref, other_near_ref)
        traces = [
            total.astype(jnp.bfloat16)
            for total in three((first_ref, second_ref), far_ref, near_ref, same_ref, others, pairs_ref)
        ]
        depth, width = dense_ref.shape[0], field_ref.shape[2]
        beside = [
            jnp.stack([ref[depth:, :width], ref[depth:, width:]]) for ref in (other_far_ref, other_near_ref)
        ]
        fields = (beside[0], field_ref[...], beside[1])
        window = [plus(field, trace) for field, trace in zip(fields, traces)]
        trace = applied(window, dense_ref).astype(jnp.bfloat16)
        down_ref[...] = trace
        if more_refs:
            send_ref, wait_ref = more_refs
            send_ref[...] = plus(next_ref[...], trace)
            wait_ref[...] = window[1]
        mid_ref[...] = traces[1]


def turn_kernel(
    layer, far_ref, near_ref, same_ref, dense_ref, below_ref, wait_ref, kept_ref, send_ref, up_ref, down_ref
):
    up_ref[...] = kept_ref[...]
    down_ref[...] = kept_ref[...]

    @pl.when(lax.axis_index("depth") == layer)
    def _():
        down_ref[...] = below_ref[...]
        window = (far_ref[...], same_ref[...], near_ref[...])
        trace = plus(below_ref[...], applied(window, dense_ref))
        up_ref[...] = trace
        send_ref[...] = plus(wait_ref[...], trace)


def up_two_kernel(
    layer, lone, first_ref, far_ref, second_ref, near_ref, same_ref, other_far_ref, other_same_ref, other_near_ref,
    dense_ref, down_ref, below_ref, wait_ref, kept_ref, other_ref, send_ref, up_ref, back_ref, pairs_ref,
):
    up_ref[...] = kept_ref[...]
    back_ref[...] = other_ref[...]

    @pl.when(lax.axis_index("depth") == layer)
    def _():
        others = (other_far_ref, other_same_ref, other_near_ref)
        totals = three((first_ref, second_ref), far_ref, near_ref, same_ref, others, pairs_ref)
        window = [total.astype(jnp.bfloat16) for total in totals]
        back_ref[...] = window[1]
        below = down_ref[...] if lone else below_ref[...]
        trace = plus(below, applied(window, dense_ref))
        up_ref[...] = trace
        send_ref[...] = trace if lone else plus(wait_ref[...], trace)


def chosen_kernel(layers, up_ref, returned_ref, out_ref):
    layer = lax.axis_index("depth")
    out_ref[...] = up_ref[...]

    @pl.when(functools.reduce(jnp.logical_or, [layer == k for k in layers]))
    def _():
        out_ref[...] = returned_ref[...]


def last_kernel(passed, far_ref, near_ref, same_ref, dense_ref, down_ref, below_ref, kept_ref, up_out_ref, down_out_ref):
    layer = lax.axis_index("depth")
    up_out_ref[...] = kept_ref[...]
    down_out_ref[...] = down_ref[...]

    @pl.when(layer == passed)
    def _():
        down_out_ref[...] = below_ref[...]

    @pl.when(layer == 0)
    def _():
        window = (far_ref[...], same_ref[...], near_ref[...])
        up_out_ref[...] = plus(down_ref[...], applied(window, dense_ref))


def vmem(count):
    return [pl.BlockSpec(memory_space=pltpu.VMEM)] * count


def local(forcing, blocks, block_rows, block_cols):
    layers, lats = lax.axis_size("depth"), lax.axis_size("lat")
    field = forcing[0]
    _, sources, width = field.shape
    count, parts, size, _ = blocks.shape[1:]
    rows = width // size
    top, split = layers - 1, layers // 2 - 1

    def sent(value, steps, place):
        pairs = [
            (k * lats + j, to_k * lats + place(j))
            for k, to_k in steps
            for j in range(lats)
            if 0 <= place(j) < lats
        ]
        return lax.ppermute(value, AXES, pairs)

    def far(j):
        return j + 1 if j % 2 else j - 1

    def near(j):
        return j - 1 if j % 2 else j + 1

    def same(j):
        return j

    def first(j):
        return j + 2 if j % 4 > 1 else j - 2

    def second(j):
        return j - 2 if j % 4 > 1 else j + 2

    rounds = [(k, k + 1) for k in range(split)] + [(k, k + 2) for k in range(split, top, 2)]
    rounds += [(top, top - 1)] + [(k, k - 2) for k in range(top - 1, 2, -2)] + [(2, 1), (1, 0)]
    wide, narrow = {step: [step] for step in rounds}, {step: [step] for step in rounds}
    if layers == 8:
        narrow |= {step: [(2, 3), (7, 6)] for step in ((2, 3), (7, 6))}
        for shared in ([(5, 7), (4, 2)], [(3, 5), (6, 4)]):
            narrow |= {step: shared for step in shared}
            wide |= {step: shared for step in shared}

    def moved(value, k, to_k):
        step = narrow[k, to_k]
        return sent(value, [(k, to_k)], far), sent(value, step, near), sent(value, step, same)

    def moved_two(value, k, to_k):
        outer, inner = wide[k, to_k], narrow[k, to_k]
        return (
            sent(value, outer, first),
            sent(value, outer, far),
            sent(value, outer, second),
            sent(value, inner, near),
            sent(value, inner, same),
        )

    following = sent(field, [(k, k - 1) for k in range(1, layers)], same)

    left_is_far = lax.axis_index("lat") % 2 == 0
    cols = jnp.where(left_is_far, block_cols, 2 * rows - block_cols // rows * rows + block_cols % rows)
    matrix = jax.ShapeDtypeStruct((3 * width, parts * width), jnp.bfloat16)
    payload = jax.ShapeDtypeStruct((3 * width + sources, parts * width), jnp.bfloat16)
    dense = pl.pallas_call(
        dense_kernel,
        out_shape=matrix,
        in_specs=[pl.BlockSpec(memory_space=pltpu.SMEM)] * 2 + vmem(1),
        out_specs=pl.BlockSpec(memory_space=pltpu.VMEM),
        scratch_shapes=[pltpu.VMEM((rows, 3 * rows, parts, size, size), jnp.float32)],
        compiler_params=PARAMS,
        name="dense",
    )(block_rows, cols, blocks[0])

    one = jax.ShapeDtypeStruct(field.shape, jnp.bfloat16)
    two = jax.ShapeDtypeStruct((2, *field.shape), jnp.bfloat16)

    def step(kernel, out_shape, layer, *operands, pairs=False):
        return pl.pallas_call(
            functools.partial(kernel, *layer),
            out_shape=out_shape,
            in_specs=vmem(len(operands)),
            out_specs=tuple(vmem(len(out_shape))),
            scratch_shapes=[pltpu.VMEM(two.shape, two.dtype)] if pairs else [],
            compiler_params=PARAMS,
            name=kernel.__name__,
        )(*operands)

    def hold(value, *others):
        return pl.pallas_call(
            hold_kernel,
            out_shape=one,
            in_specs=vmem(1) + [pl.BlockSpec(memory_space=pl.ANY)] * len(others),
            out_specs=pl.BlockSpec(memory_space=pltpu.VMEM),
            compiler_params=PARAMS,
            name="hold",
        )(value, *others)

    ups = [(k + 1, k) for k in range(2, top - 1, 2)]
    downs = [(k, k + 1) for k in range(split + 1, top, 2)]
    given = [*ups, *downs]
    send, down = field, jnp.zeros(field.shape, jnp.bfloat16)
    window = (sent(field, [(0, 0)], far), sent(field, [(0, 0)], near), field)
    for layer in range(split + 1):
        if layer == 1:
            following = hold(following, other_same)
        if layer == split:
            following = hold(following, other_near)
        shift = 1 if layer == 2 else 0
        parts = [*window[shift:], *window[:shift]]
        send, down = step(down_kernel, (one, one), (layer, shift), following, *parts, dense, down, send)
        if layer < split:
            window = moved(send, layer, layer + 1)
        if layer == 0:
            [load] = step(later_kernel, (payload,), ([k for k, _ in given],), dense, following, send)
            other_far, other_near, other_same = (sent(load, given, place) for place in (far, near, same))
    mid = jnp.zeros(field.shape, jnp.bfloat16)
    for layer in range(split + 2, top + 1, 2):
        following = hold(following, other_far) if layer < top else following
        window = moved_two(send, layer - 2, layer)
        down, mid, *more = step(
            down_two_kernel, (one,) * (4 if layer < top else 2), (layer,), *window,
            other_far, other_same, other_near, dense, field, following, down, send, mid, pairs=True,
        )
        if layer < top:
            send, kept = more
            wait = sent(kept, [(2, 4), (5, 6)], same)
    window = moved(down, top, top - 1)
    below = sent(mid, [(5, 4), (7, 6)], same)
    send, up, down = step(turn_kernel, (one,) * 3, (top - 1,), *window, dense, below, wait, down)
    back = jnp.zeros(field.shape, jnp.bfloat16)
    for layer in range(top - 3, 1, -2):
        window = moved_two(send, layer + 2, layer)
        send, up, back = step(
            up_two_kernel, (one,) * 3, (layer, layer == 2), *window, other_far, other_same, other_near, dense,
            down, below, wait, up, back, pairs=True,
        )
    returned = sent(back, [(to_k, k) for k, to_k in ups], same)
    [up] = step(up_kernel, (one,), (1,), *moved(send, 2, 1), dense, down, up)
    [up] = step(chosen_kernel, (one,), ([k for k, _ in ups],), up, returned)
    up, down = step(last_kernel, (one, one), (split + 1,), *moved(up, 1, 0), dense, down, below, up)
    return (down.reshape(forcing.shape), up.reshape(forcing.shape))


def solution(mesh):
    placed = (
        P("depth", None, None, "lat"),
        P("depth", "lat", None, None, None),
        P("depth", "lat"),
        P("depth", "lat"),
    )
    return jax.shard_map(
        local,
        mesh=mesh,
        in_specs=placed,
        out_specs=(P("depth", None, None, "lat"), P("depth", None, None, "lat")),
        check_vma=False,
    )
```

```python
import functools

import jax
import jax.numpy as jnp
from jax import lax
from jax.experimental import pallas as pl
from jax.experimental.pallas import tpu as pltpu
from jax.sharding import PartitionSpec as P

AXES = ("depth", "lat")
PARAMS = pltpu.CompilerParams(vmem_limit_bytes=24 * 2**20)


def dense_kernel(rows_ref, cols_ref, blocks_ref, dense_ref, total_ref):
    count, parts, size, _ = blocks_ref.shape
    rows, slots = total_ref.shape[:2]
    total_ref[...] = jnp.zeros_like(total_ref)
    for b in range(count):
        total_ref[rows_ref[0, b], cols_ref[0, b]] += blocks_ref[b].astype(jnp.float32)
    for r in range(rows):
        for s in range(slots):
            for p in range(parts):
                column = (p * rows + r) * size
                dense_ref[s * size : (s + 1) * size, column : column + size] = (
                    total_ref[r, s, p].T.astype(jnp.bfloat16)
                )


def hold_kernel(field_ref, *refs):
    refs[-1][...] = field_ref[...]


def later_kernel(layers, dense_ref, next_ref, _after, load_ref):
    layer = lax.axis_index("depth")
    depth, width = dense_ref.shape[0], next_ref.shape[2]

    @pl.when(functools.reduce(jnp.logical_or, [layer == k for k in layers]))
    def _():
        load_ref[:depth] = dense_ref[...]
        load_ref[depth:, :width] = next_ref[0]
        load_ref[depth:, width:] = next_ref[1]


def up_kernel(layer, far_ref, near_ref, same_ref, dense_ref, down_ref, kept_ref, up_ref):
    up_ref[...] = kept_ref[...]

    @pl.when(lax.axis_index("depth") == layer)
    def _():
        window = (far_ref[...], same_ref[...], near_ref[...])
        up_ref[...] = plus(down_ref[...], applied(window, dense_ref))


def applied(window, dense_ref):
    sources, width = window[0].shape[1:]
    flat = jnp.concatenate([part.reshape(2 * sources, width) for part in window], axis=1)
    product = jnp.dot(flat, dense_ref[: flat.shape[1]], preferred_element_type=jnp.float32)
    by_real, by_imag = product[:, :width], product[:, width:]
    real = by_real[:sources] - by_imag[sources:]
    imag = by_real[sources:] + by_imag[:sources]
    return jnp.stack([real, imag])


def plus(field, trace):
    return (field.astype(jnp.float32) + trace.astype(jnp.float32)).astype(jnp.bfloat16)


def three(outer, far_ref, near_ref, same_ref, dense_refs, pairs_ref):
    first_ref, second_ref = outer
    place = lax.axis_index("lat") % 4
    first_is_far = (place == 0) | (place == 3)

    @pl.when(first_is_far)
    def _():
        pairs_ref[0] = first_ref[...]
        pairs_ref[1] = second_ref[...]

    @pl.when(jnp.logical_not(first_is_far))
    def _():
        pairs_ref[0] = second_ref[...]
        pairs_ref[1] = first_ref[...]

    far, near, same = far_ref[...], near_ref[...], same_ref[...]
    return (
        applied((same, far, pairs_ref[0]), dense_refs[0]),
        applied((far, same, near), dense_refs[1]),
        applied((pairs_ref[1], near, same), dense_refs[2]),
    )


def down_kernel(layer, shift, next_ref, *refs):
    *window_refs, dense_ref, kept_ref, sent_ref, send_ref, down_ref = refs
    far_ref, near_ref, same_ref = window_refs[-shift:] + window_refs[:-shift] if shift else window_refs
    down_ref[...] = kept_ref[...]
    send_ref[...] = sent_ref[...]

    @pl.when(lax.axis_index("depth") == layer)
    def _():
        window = (far_ref[...], same_ref[...], near_ref[...])
        trace = applied(window, dense_ref).astype(jnp.bfloat16)
        down_ref[...] = trace
        send_ref[...] = plus(next_ref[...], trace)


def down_two_kernel(
    layer, swapped, first_ref, far_ref, second_ref, near_ref, same_ref, other_far_ref, other_same_ref, other_near_ref,
    dense_ref, field_ref, next_ref, kept_ref, sent_ref, passed_ref, down_ref, mid_ref, *rest,
):
    if swapped:
        first_ref, far_ref = far_ref, first_ref
    *more_refs, pairs_ref = rest
    down_ref[...] = kept_ref[...]
    mid_ref[...] = passed_ref[...]
    for ref in more_refs[1:]:
        ref[...] = sent_ref[...]

    @pl.when(lax.axis_index("depth") == layer)
    def _():
        others = (other_far_ref, other_same_ref, other_near_ref)
        traces = [
            total.astype(jnp.bfloat16)
            for total in three((first_ref, second_ref), far_ref, near_ref, same_ref, others, pairs_ref)
        ]
        depth, width = dense_ref.shape[0], field_ref.shape[2]
        beside = [
            jnp.stack([ref[depth:, :width], ref[depth:, width:]]) for ref in (other_far_ref, other_near_ref)
        ]
        fields = (beside[0], field_ref[...], beside[1])
        window = [plus(field, trace) for field, trace in zip(fields, traces)]
        trace = applied(window, dense_ref).astype(jnp.bfloat16)
        down_ref[...] = trace
        if more_refs:
            send_ref, wait_ref = more_refs
            send_ref[...] = plus(next_ref[...], trace)
            wait_ref[...] = window[1]
        mid_ref[...] = traces[1]


def turn_kernel(
    layer, far_ref, near_ref, same_ref, dense_ref, below_ref, wait_ref, kept_ref, send_ref, up_ref, down_ref
):
    up_ref[...] = kept_ref[...]
    down_ref[...] = kept_ref[...]

    @pl.when(lax.axis_index("depth") == layer)
    def _():
        down_ref[...] = below_ref[...]
        window = (far_ref[...], same_ref[...], near_ref[...])
        trace = plus(below_ref[...], applied(window, dense_ref))
        up_ref[...] = trace
        send_ref[...] = plus(wait_ref[...], trace)


def up_two_kernel(
    layer, lone, swapped, first_ref, far_ref, second_ref, near_ref, same_ref, other_far_ref, other_same_ref, other_near_ref,
    dense_ref, down_ref, below_ref, wait_ref, kept_ref, other_ref, send_ref, up_ref, back_ref, pairs_ref,
):
    if swapped:
        first_ref, far_ref = far_ref, first_ref
    up_ref[...] = kept_ref[...]
    back_ref[...] = other_ref[...]

    @pl.when(lax.axis_index("depth") == layer)
    def _():
        others = (other_far_ref, other_same_ref, other_near_ref)
        totals = three((first_ref, second_ref), far_ref, near_ref, same_ref, others, pairs_ref)
        window = [total.astype(jnp.bfloat16) for total in totals]
        back_ref[...] = window[1]
        below = down_ref[...] if lone else below_ref[...]
        trace = plus(below, applied(window, dense_ref))
        up_ref[...] = trace
        send_ref[...] = trace if lone else plus(wait_ref[...], trace)


def chosen_kernel(layers, up_ref, returned_ref, out_ref):
    layer = lax.axis_index("depth")
    out_ref[...] = up_ref[...]

    @pl.when(functools.reduce(jnp.logical_or, [layer == k for k in layers]))
    def _():
        out_ref[...] = returned_ref[...]


def last_kernel(passed, far_ref, near_ref, same_ref, dense_ref, down_ref, below_ref, kept_ref, up_out_ref, down_out_ref):
    layer = lax.axis_index("depth")
    up_out_ref[...] = kept_ref[...]
    down_out_ref[...] = down_ref[...]

    @pl.when(layer == passed)
    def _():
        down_out_ref[...] = below_ref[...]

    @pl.when(layer == 0)
    def _():
        window = (far_ref[...], same_ref[...], near_ref[...])
        up_out_ref[...] = plus(down_ref[...], applied(window, dense_ref))


def vmem(count):
    return [pl.BlockSpec(memory_space=pltpu.VMEM)] * count


def local(forcing, blocks, block_rows, block_cols):
    layers, lats = lax.axis_size("depth"), lax.axis_size("lat")
    field = forcing[0]
    _, sources, width = field.shape
    count, parts, size, _ = blocks.shape[1:]
    rows = width // size
    top, split = layers - 1, layers // 2 - 1

    def sent(value, steps, place):
        pairs = [
            (k * lats + j, to_k * lats + place(j))
            for k, to_k in steps
            for j in range(lats)
            if 0 <= place(j) < lats
        ]
        return lax.ppermute(value, AXES, pairs)

    def far(j):
        return j + 1 if j % 2 else j - 1

    def near(j):
        return j - 1 if j % 2 else j + 1

    def same(j):
        return j

    def first(j):
        return j + 2 if j % 4 > 1 else j - 2

    def second(j):
        return j - 2 if j % 4 > 1 else j + 2

    rounds = [(k, k + 1) for k in range(split)] + [(k, k + 2) for k in range(split, top, 2)]
    rounds += [(top, top - 1)] + [(k, k - 2) for k in range(top - 1, 2, -2)] + [(2, 1), (1, 0)]
    wide, narrow = {step: [step] for step in rounds}, {step: [step] for step in rounds}
    if layers == 8:
        narrow |= {step: [(2, 3), (7, 6)] for step in ((2, 3), (7, 6))}
        for shared in ([(5, 7), (4, 2)], [(3, 5), (6, 4)]):
            narrow |= {step: shared for step in shared}
            wide |= {step: shared for step in shared}

    def moved(value, k, to_k):
        step = narrow[k, to_k]
        return sent(value, [(k, to_k)], far), sent(value, step, near), sent(value, step, same)

    def moved_two(value, k, to_k):
        outer, inner = wide[k, to_k], narrow[k, to_k]
        long = [sent(value, outer, first), sent(value, outer, far)]
        return (
            *(long[::-1] if to_k in (2, top) else long),
            sent(value, outer, second),
            sent(value, inner, near),
            sent(value, inner, same),
        )

    following = sent(field, [(k, k - 1) for k in range(1, layers)], same)

    left_is_far = lax.axis_index("lat") % 2 == 0
    cols = jnp.where(left_is_far, block_cols, 2 * rows - block_cols // rows * rows + block_cols % rows)
    matrix = jax.ShapeDtypeStruct((3 * width, parts * width), jnp.bfloat16)
    payload = jax.ShapeDtypeStruct((3 * width + sources, parts * width), jnp.bfloat16)
    dense = pl.pallas_call(
        dense_kernel,
        out_shape=matrix,
        in_specs=[pl.BlockSpec(memory_space=pltpu.SMEM)] * 2 + vmem(1),
        out_specs=pl.BlockSpec(memory_space=pltpu.VMEM),
        scratch_shapes=[pltpu.VMEM((rows, 3 * rows, parts, size, size), jnp.float32)],
        compiler_params=PARAMS,
        name="dense",
    )(block_rows, cols, blocks[0])

    one = jax.ShapeDtypeStruct(field.shape, jnp.bfloat16)
    two = jax.ShapeDtypeStruct((2, *field.shape), jnp.bfloat16)

    def step(kernel, out_shape, layer, *operands, pairs=False):
        return pl.pallas_call(
            functools.partial(kernel, *layer),
            out_shape=out_shape,
            in_specs=vmem(len(operands)),
            out_specs=tuple(vmem(len(out_shape))),
            scratch_shapes=[pltpu.VMEM(two.shape, two.dtype)] if pairs else [],
            compiler_params=PARAMS,
            name=kernel.__name__,
        )(*operands)

    def hold(value, *others):
        return pl.pallas_call(
            hold_kernel,
            out_shape=one,
            in_specs=vmem(1) + [pl.BlockSpec(memory_space=pl.ANY)] * len(others),
            out_specs=pl.BlockSpec(memory_space=pltpu.VMEM),
            compiler_params=PARAMS,
            name="hold",
        )(value, *others)

    ups = [(k + 1, k) for k in range(2, top - 1, 2)]
    downs = [(k, k + 1) for k in range(split + 1, top, 2)]
    given = [*ups, *downs]
    send, down = field, jnp.zeros(field.shape, jnp.bfloat16)
    window = (sent(field, [(0, 0)], far), sent(field, [(0, 0)], near), field)
    for layer in range(split + 1):
        if layer == 1:
            following = hold(following, other_same)
        if layer == split:
            following = hold(following, other_near)
        shift = 1 if layer == 2 else 0
        parts = [*window[shift:], *window[:shift]]
        send, down = step(down_kernel, (one, one), (layer, shift), following, *parts, dense, down, send)
        if layer < split:
            window = moved(send, layer, layer + 1)
        if layer == 0:
            [load] = step(later_kernel, (payload,), ([k for k, _ in given],), dense, following, send)
            other_far, other_near, other_same = (sent(load, given, place) for place in (far, near, same))
    mid = jnp.zeros(field.shape, jnp.bfloat16)
    for layer in range(split + 2, top + 1, 2):
        following = hold(following, other_far) if layer < top else following
        window = moved_two(send, layer - 2, layer)
        down, mid, *more = step(
            down_two_kernel, (one,) * (4 if layer < top else 2), (layer, layer == top), *window,
            other_far, other_same, other_near, dense, field, following, down, send, mid, pairs=True,
        )
        if layer < top:
            send, kept = more
            wait = sent(kept, [(2, 4), (5, 6)], same)
    window = moved(down, top, top - 1)
    below = sent(mid, [(5, 4), (7, 6)], same)
    send, up, down = step(turn_kernel, (one,) * 3, (top - 1,), *window, dense, below, wait, down)
    back = jnp.zeros(field.shape, jnp.bfloat16)
    for layer in range(top - 3, 1, -2):
        window = moved_two(send, layer + 2, layer)
        send, up, back = step(
            up_two_kernel, (one,) * 3, (layer, layer == 2, layer == 2), *window, other_far, other_same, other_near, dense,
            down, below, wait, up, back, pairs=True,
        )
    returned = sent(back, [(to_k, k) for k, to_k in ups], same)
    [up] = step(up_kernel, (one,), (1,), *moved(send, 2, 1), dense, down, up)
    [up] = step(chosen_kernel, (one,), ([k for k, _ in ups],), up, returned)
    up, down = step(last_kernel, (one, one), (split + 1,), *moved(up, 1, 0), dense, down, below, up)
    return (down.reshape(forcing.shape), up.reshape(forcing.shape))


def solution(mesh):
    placed = (
        P("depth", None, None, "lat"),
        P("depth", "lat", None, None, None),
        P("depth", "lat"),
        P("depth", "lat"),
    )
    return jax.shard_map(
        local,
        mesh=mesh,
        in_specs=placed,
        out_specs=(P("depth", None, None, "lat"), P("depth", None, None, "lat")),
        check_vma=False,
    )
```
